512 devices in a mesh: img: 32 (over x, y), ref: 16 (over z, core).
Axes of the slice: x: 4, y: 8, z: 8, core: 2. Of those that a mesh axis runs over, the one named last changes fastest.
Arguments:
- images: bfloat16 [32768, 2048], P('img'), may hold values from -8 to 8
- references: bfloat16 [8192, 2048], P('ref'), may hold values from -1 to 1
- initial_contrast: float32 [32768], P('img'), may hold values from 0.25 to 1.75
Outputs:
- new_references: bfloat16 [8192, 2048], P('ref')
- contrast: float32 [32768], P('img')
- loglik: float32 [32768], P('img')
The draws below stay inside these ranges and needn't reach their ends.
All inputs are finite; a program needn't handle non-finite values.
Results may differ from the reference program's by a relative error of at most 0.0041.
Values may be sent and summed in bfloat16 or wider, within the bound.
No kernel may reach another device: no remote copies, remote signals or barrier semaphores. Data moves between devices by JAX's collectives and lax.ppermute only.
A program may use at most 64 MiB of HBM per device.

```python
import math
import jax
import jax.numpy as jnp
from jax import lax

F = 2048
IMG_DEV = 1024
ITERS = 3
NIMG = 32768
NREF = 8192


def ref_table(key):
    subkey = jax.random.fold_in(key, 11)
    gaussian = jnp.clip(jax.random.normal(subkey, (NREF, F), jnp.float32), -4.0, 4.0)
    row_scale = 0.6 + 1.2 * jnp.arange(NREF, dtype=jnp.float32) / NREF
    return gaussian * row_scale[:, None] * F ** (-0.5)


def draw_references(key, part):
    return ref_table(key).astype(jnp.bfloat16)


def draw_images(key, part):
    subkey = jax.random.fold_in(key, 23)
    gaussian = jax.random.normal(subkey, (NIMG, F), jnp.float32)
    return jnp.clip(gaussian, -8.0, 8.0).astype(jnp.bfloat16)


def setup_inputs(seed: int = 0) -> dict:
    key_of = jax.random.split(jax.random.key(seed), 4)
    images = draw_images(jax.random.fold_in(key_of[3], 71), 0)
    references = draw_references(jax.random.fold_in(key_of[3], 71), 0)
    initial_contrast = jnp.clip(1.0 + 0.15 * jax.random.normal(key_of[2], (NIMG,), jnp.float32), 0.25, 1.75)
    return {"images": images, "references": references, "initial_contrast": initial_contrast}


sharpness = 2.0
prior_weight = 1.0
epsilon = 1e-06

def scores_of(cross_terms, ref_norms, contrast):
    contrast_col = contrast[:, None]
    return sharpness * (contrast_col * cross_terms - 0.5 * (contrast_col * contrast_col) * ref_norms[None, :])

def statistics(cross_terms, ref_norms, contrast):
    scored = scores_of(cross_terms, ref_norms, contrast)
    highest = lax.optimization_barrier(jnp.max(scored, axis=1))
    exponent = jnp.exp(scored - highest[:, None])
    summed = lax.optimization_barrier(jnp.sum(exponent, axis=1))
    weighted_cross = lax.optimization_barrier(jnp.sum(exponent * cross_terms, axis=1))
    weighted_norm = lax.optimization_barrier(jnp.sum(exponent * ref_norms[None, :], axis=1))
    return (highest, summed, weighted_cross, weighted_norm, exponent)

def normalize(sums):
    meansq = lax.optimization_barrier(jnp.mean(sums * sums, axis=1))
    return (sums * lax.rsqrt(meansq + epsilon)[:, None]).astype(jnp.bfloat16)

def reference(images, references, initial_contrast):
    ref_norms = lax.optimization_barrier(jnp.sum(jnp.square(references.astype(jnp.float32)), axis=1))
    image_blocks = images.reshape(NIMG // IMG_DEV, IMG_DEV, F)
    prior_blocks = initial_contrast.reshape(NIMG // IMG_DEV, IMG_DEV)

    def one_block(running, carried):
        image_block, prior = carried
        cross_terms = lax.dot_general(image_block, references, (((1,), (1,)), ((), ())), preferred_element_type=jnp.float32)
        contrast = prior
        for iteration in range(ITERS + 1):
            highest, summed, weighted_cross, weighted_norm, exponent = statistics(cross_terms, ref_norms, contrast)
            if iteration < ITERS:
                contrast = (weighted_cross / summed + prior_weight * prior) / (weighted_norm / summed + prior_weight)
        posterior = exponent / summed[:, None]
        weights = (posterior * contrast[:, None]).astype(jnp.bfloat16)
        running = running + lax.dot_general(weights, image_block, (((0,), (0,)), ((), ())), preferred_element_type=jnp.float32)
        return (running, contrast)
    sums, contrasts = lax.scan(one_block, jnp.zeros((NREF, F), jnp.float32), (image_blocks, prior_blocks))
    new_references = normalize(sums)
    new_norms = lax.optimization_barrier(jnp.sum(jnp.square(new_references.astype(jnp.float32)), axis=1)) / F

    def rescore(carried):
        image_block, contrast = carried
        new_cross = lax.dot_general(image_block, new_references, (((1,), (1,)), ((), ())), preferred_element_type=jnp.float32) * F ** (-0.5)
        highest, summed, weighted_cross, weighted_norm, exponent = statistics(new_cross, new_norms, contrast)
        return highest + jnp.log(summed) - math.log(NREF)
    loglik = lax.map(rescore, (image_blocks, contrasts))
    return (new_references, contrasts.reshape(NIMG), loglik.reshape(NIMG))
```

```python
import math

import jax
import jax.numpy as jnp
from jax import lax
from jax.sharding import PartitionSpec as P

ITERS = 3


sharpness = 2.0
prior_weight = 1.0
epsilon = 1e-06


def sent_to_all(value, axis):
    devices = lax.axis_size(axis)
    return lax.all_to_all(
        jnp.broadcast_to(value[None], (devices, *value.shape)), axis, 0, 0, tiled=True
    )


def scores_of(cross_terms, ref_norms, contrast):
    contrast_col = contrast[:, None]
    return sharpness * (
        contrast_col * cross_terms - 0.5 * (contrast_col * contrast_col) * ref_norms[None, :]
    )


def statistics(cross_terms, ref_norms, contrast, weighted=True):
    scored = scores_of(cross_terms, ref_norms, contrast)
    own_high = jnp.max(scored, axis=1)
    exponent = jnp.exp(scored - own_high[:, None])
    rows = [own_high, jnp.sum(exponent, axis=1)]
    if weighted:
        rows.append(jnp.sum(exponent * cross_terms, axis=1))
        rows.append(jnp.sum(exponent * ref_norms[None, :], axis=1))
    everything = sent_to_all(jnp.stack(rows), "ref")
    highest = jnp.max(everything[:, 0], axis=0)
    scale = jnp.exp(everything[:, 0] - highest[None])
    sums = jnp.sum(everything[:, 1:] * scale[:, None], axis=0)
    return highest, sums, exponent, jnp.exp(own_high - highest)


def normalize(sums):
    meansq = jnp.mean(sums * sums, axis=1)
    return (sums * lax.rsqrt(meansq + epsilon)[:, None]).astype(jnp.bfloat16)


def per_device(images, references, initial_contrast):
    ref_norms = jnp.sum(jnp.square(references.astype(jnp.float32)), axis=1)
    cross_terms = lax.dot_general(
        images, references, (((1,), (1,)), ((), ())), preferred_element_type=jnp.float32
    )
    contrast = initial_contrast
    for _ in range(ITERS):
        _, (summed, along, weight), _, _ = statistics(cross_terms, ref_norms, contrast)
        contrast = (along / summed + prior_weight * initial_contrast) / (
            weight / summed + prior_weight
        )
    _, (summed,), exponent, scale = statistics(cross_terms, ref_norms, contrast, False)
    weights = (exponent * (scale / summed * contrast)[:, None]).astype(jnp.bfloat16)
    img_partial = lax.dot_general(
        weights, images, (((0,), (0,)), ((), ())), preferred_element_type=jnp.float32
    )
    size = lax.axis_size("img")
    refs, width = img_partial.shape
    pieces = img_partial.astype(jnp.bfloat16).reshape(size, refs // size, width)
    pieces = lax.all_to_all(pieces, "img", 0, 0, tiled=True)
    mine = normalize(jnp.sum(pieces.astype(jnp.float32), axis=0))
    gathered = sent_to_all(mine, "img").reshape(refs, width)
    new_norms = jnp.sum(jnp.square(gathered.astype(jnp.float32)), axis=1) / width
    new_cross = lax.dot_general(
        images, gathered, (((1,), (1,)), ((), ())), preferred_element_type=jnp.float32
    ) * width ** (-0.5)
    final_high, (final_sum,), _, _ = statistics(new_cross, new_norms, contrast, False)
    loglik = final_high + jnp.log(final_sum) - math.log(refs * lax.axis_size("ref"))
    return (gathered, contrast, loglik)


def solution(mesh):
    placed = (P("img", None), P("ref", None), P("img"))
    return jax.shard_map(
        per_device,
        mesh=mesh,
        in_specs=placed,
        out_specs=(P("ref", None), P("img"), P("img")),
        check_vma=False,
    )
```

```python
import math

import jax
import jax.numpy as jnp
from jax import lax
from jax.sharding import PartitionSpec as P

ITERS = 3


sharpness = 2.0
prior_weight = 1.0
epsilon = 1e-06


X, Y = 4, 8
NEAR = [[x * Y + 2 * pair + side for x in range(X) for side in range(2)] for pair in range(Y // 2)]
FAR = [[x * Y + 2 * pair + side for pair in range(Y // 2)] for x in range(X) for side in range(2)]


def exchanged(pieces, axis, groups=None):
    return lax.all_to_all(pieces, axis, 0, 0, tiled=True, axis_index_groups=groups)


def sent_to_all(value, axis, groups=None):
    devices = len(groups[0]) if groups else lax.axis_size(axis)
    return exchanged(jnp.broadcast_to(value[None], (devices, *value.shape)), axis, groups)


def summed_share(partial):
    rows, width = partial.shape
    for groups in (NEAR, FAR):
        rows //= len(groups[0])
        pieces = partial.astype(jnp.bfloat16).reshape(len(groups[0]), rows, width)
        partial = jnp.sum(exchanged(pieces, "img", groups).astype(jnp.float32), axis=0)
    return partial


def gathered_rows(share):
    for groups in (FAR, NEAR):
        share = sent_to_all(share, "img", groups).reshape(-1, share.shape[-1])
    return share


def scores_of(cross_terms, ref_norms, contrast):
    contrast_col = contrast[:, None]
    return sharpness * (
        contrast_col * cross_terms - 0.5 * (contrast_col * contrast_col) * ref_norms[None, :]
    )


def statistics(cross_terms, ref_norms, contrast, weighted=True):
    scored = scores_of(cross_terms, ref_norms, contrast)
    own_high = jnp.max(scored, axis=1)
    exponent = jnp.exp(scored - own_high[:, None])
    own_sum = jnp.sum(exponent, axis=1)
    own_log = own_high + jnp.log(own_sum)
    if not weighted:
        logs = sent_to_all(own_log[None], "ref")[:, 0]
        highest = jnp.max(logs, axis=0)
        log_total = highest + jnp.log(jnp.sum(jnp.exp(logs - highest[None]), axis=0))
        return log_total, exponent, own_high
    own = jnp.concatenate(
        [
            own_log,
            jnp.sum(exponent * cross_terms, axis=1) / own_sum,
            jnp.sum(exponent * ref_norms[None, :], axis=1) / own_sum,
        ]
    )
    logs, along, weight = jnp.split(sent_to_all(own[None], "ref")[:, 0], 3, axis=1)
    share = jnp.exp(logs - jnp.max(logs, axis=0)[None])
    total = jnp.sum(share, axis=0)
    return jnp.sum(share * along, axis=0) / total, jnp.sum(share * weight, axis=0) / total


def normalize(sums):
    meansq = jnp.mean(sums * sums, axis=1)
    return (sums * lax.rsqrt(meansq + epsilon)[:, None]).astype(jnp.bfloat16)


def per_device(images, references, initial_contrast):
    ref_norms = jnp.sum(jnp.square(references.astype(jnp.float32)), axis=1)
    cross_terms = lax.dot_general(
        images, references, (((1,), (1,)), ((), ())), preferred_element_type=jnp.float32
    )
    contrast = initial_contrast
    for _ in range(ITERS):
        along, weight = statistics(cross_terms, ref_norms, contrast)
        contrast = (along + prior_weight * initial_contrast) / (weight + prior_weight)
    log_total, exponent, own_high = statistics(cross_terms, ref_norms, contrast, False)
    factor = jnp.exp(own_high - log_total) * contrast
    weights = (exponent * factor[:, None]).astype(jnp.bfloat16)
    img_partial = lax.dot_general(
        weights, images, (((0,), (0,)), ((), ())), preferred_element_type=jnp.float32
    )
    gathered = gathered_rows(normalize(summed_share(img_partial)))
    refs, width = gathered.shape
    new_norms = jnp.sum(jnp.square(gathered.astype(jnp.float32)), axis=1) / width
    new_cross = lax.dot_general(
        images, gathered, (((1,), (1,)), ((), ())), preferred_element_type=jnp.float32
    ) * width ** (-0.5)
    log_total, _, _ = statistics(new_cross, new_norms, contrast, False)
    loglik = log_total - math.log(refs * lax.axis_size("ref"))
    return (gathered, contrast, loglik)


def solution(mesh):
    placed = (P("img", None), P("ref", None), P("img"))
    return jax.shard_map(
        per_device,
        mesh=mesh,
        in_specs=placed,
        out_specs=(P("ref", None), P("img"), P("img")),
        check_vma=False,
    )
```

```python
import math

import jax
import jax.numpy as jnp
from jax import lax
from jax.sharding import PartitionSpec as P

ITERS = 3


sharpness = 2.0
prior_weight = 1.0
epsilon = 1e-06


X, Y = 4, 8
DISTANCES = (2, 1, 3)
COLUMNS = [[x * Y + y for y in range(Y)] for x in range(X)]


def exchanged(pieces, axis, groups=None):
    return lax.all_to_all(pieces, axis, 0, 0, tiled=True, axis_index_groups=groups)


def sent_to_all(value, axis, groups=None):
    devices = len(groups[0]) if groups else lax.axis_size(axis)
    return exchanged(jnp.broadcast_to(value[None], (devices, *value.shape)), axis, groups)


def along_x(value, distance):
    return lax.ppermute(value, "img", [(i, (i + distance * Y) % (X * Y)) for i in range(X * Y)])


def scores_of(cross_terms, ref_norms, contrast):
    contrast_col = contrast[:, None]
    return sharpness * (
        contrast_col * cross_terms - 0.5 * (contrast_col * contrast_col) * ref_norms[None, :]
    )


def relative(cross_terms, ref_norms, contrast):
    scored = scores_of(cross_terms, ref_norms, contrast)
    own_high = jnp.max(scored, axis=1)
    return jnp.exp(scored - own_high[:, None]), own_high


def refitted(cross_terms, ref_norms, contrast, prior):
    exponent, own_high = relative(cross_terms, ref_norms, contrast)
    upper = jnp.sum(exponent * (cross_terms + prior_weight * prior[:, None]), axis=1)
    lower = jnp.sum(exponent * (ref_norms + prior_weight)[None, :], axis=1)
    own = jnp.concatenate([own_high + jnp.log(lower), upper / lower])
    logs, quotients = jnp.split(sent_to_all(own[None], "ref")[:, 0], 2, axis=1)
    share = jnp.exp(logs - jnp.max(logs, axis=0)[None])
    return jnp.sum(share * quotients, axis=0) / jnp.sum(share, axis=0)


def log_total(own_log):
    logs = sent_to_all(own_log[None], "ref")[:, 0]
    highest = jnp.max(logs, axis=0)
    return highest + jnp.log(jnp.sum(jnp.exp(logs - highest[None]), axis=0))


def normalize(sums):
    meansq = jnp.mean(sums * sums, axis=1)
    return (sums * lax.rsqrt(meansq + epsilon)[:, None]).astype(jnp.bfloat16)


def per_device(images, references, initial_contrast):
    ref_norms = jnp.sum(jnp.square(references.astype(jnp.float32)), axis=1)
    cross_terms = lax.dot_general(
        images, references, (((1,), (1,)), ((), ())), preferred_element_type=jnp.float32
    )
    contrast = initial_contrast
    for _ in range(ITERS):
        contrast = refitted(cross_terms, ref_norms, contrast, initial_contrast)
    exponent, own_high = relative(cross_terms, ref_norms, contrast)
    total = log_total(own_high + jnp.log(jnp.sum(exponent, axis=1)))
    factor = jnp.exp(own_high - total) * contrast
    weights = (exponent * factor[:, None]).astype(jnp.bfloat16)

    refs, width = references.shape
    rows = refs // X
    x = lax.div(lax.axis_index("img"), Y)

    def partial_of(x):
        chosen = lax.dynamic_slice_in_dim(weights, x * rows, rows, 1)
        return lax.dot_general(
            chosen, images, (((0,), (0,)), ((), ())), preferred_element_type=jnp.float32
        )

    arrived = [
        along_x(partial_of(lax.rem(x + d, X)).astype(jnp.bfloat16), d) for d in DISTANCES
    ]
    partial = partial_of(x)
    for piece in arrived:
        partial = partial + piece.astype(jnp.float32)
    pieces = partial.astype(jnp.bfloat16).reshape(Y, rows // Y, width)
    sums = jnp.sum(exchanged(pieces, "img", COLUMNS).astype(jnp.float32), axis=0)

    own = sent_to_all(normalize(sums), "img", COLUMNS).reshape(rows, width)
    held = [(x, own)] + [(lax.rem(x + X - d, X), along_x(own, d)) for d in DISTANCES]
    gathered = jnp.zeros((refs, width), jnp.bfloat16)
    own_logs = []
    for at, piece in held:
        gathered = lax.dynamic_update_slice_in_dim(gathered, piece, at * rows, 0)
        new_norms = jnp.sum(jnp.square(piece.astype(jnp.float32)), axis=1) / width
        new_cross = lax.dot_general(
            images, piece, (((1,), (1,)), ((), ())), preferred_element_type=jnp.float32
        ) * width ** (-0.5)
        exponent, own_high = relative(new_cross, new_norms, contrast)
        own_logs.append(own_high + jnp.log(jnp.sum(exponent, axis=1)))
    own_logs = jnp.stack(own_logs)
    highest = jnp.max(own_logs, axis=0)
    own_log = highest + jnp.log(jnp.sum(jnp.exp(own_logs - highest[None]), axis=0))
    loglik = log_total(own_log) - math.log(refs * lax.axis_size("ref"))
    return (gathered, contrast, loglik)


def solution(mesh):
    placed = (P("img", None), P("ref", None), P("img"))
    return jax.shard_map(
        per_device,
        mesh=mesh,
        in_specs=placed,
        out_specs=(P("ref", None), P("img"), P("img")),
        check_vma=False,
    )
```

```python
import math

import jax
import jax.numpy as jnp
from jax import lax
from jax.experimental import pallas as pl
from jax.experimental.pallas import tpu as pltpu
from jax.sharding import PartitionSpec as P

ITERS = 3


sharpness = 2.0
prior_weight = 1.0
epsilon = 1e-06

X, Y = 4, 8
NEAR = [[x * Y + 2 * pair + side for x in range(X) for side in range(2)] for pair in range(Y // 2)]
FAR = [[x * Y + 2 * pair + side for pair in range(Y // 2)] for x in range(X) for side in range(2)]


def exchanged(pieces, axis, groups=None):
    return lax.all_to_all(pieces, axis, 0, 0, tiled=True, axis_index_groups=groups)


def sent_to_all(value, axis, groups=None):
    devices = len(groups[0]) if groups else lax.axis_size(axis)
    return exchanged(jnp.broadcast_to(value[None], (devices, *value.shape)), axis, groups)


def summed_share(partial):
    rows, width = partial.shape
    for groups in (NEAR, FAR):
        rows //= len(groups[0])
        pieces = partial.astype(jnp.bfloat16).reshape(len(groups[0]), rows, width)
        partial = jnp.sum(exchanged(pieces, "img", groups).astype(jnp.float32), axis=0)
    return partial


def gathered_rows(share):
    for groups in (FAR, NEAR):
        share = sent_to_all(share, "img", groups).reshape(-1, share.shape[-1])
    return share


def normalize(sums):
    meansq = jnp.mean(sums * sums, axis=1)
    return (sums * lax.rsqrt(meansq + epsilon)[:, None]).astype(jnp.bfloat16)


LANES = 128
GROUP = 4


def spread(value, group):
    rows = [
        jnp.broadcast_to(value[k : k + 1], (8, LANES))
        for k in range(group * GROUP, (group + 1) * GROUP)
    ]
    return jnp.concatenate(rows, axis=1)


def folded(parts):
    rows = [part[:, k * LANES : (k + 1) * LANES] for part in parts for k in range(GROUP)]
    return jnp.concatenate(rows, axis=0)


def scan_rows(cross, norms, group, contrast, body, init, rows=8, unroll=8):
    twice = sharpness * spread(contrast, group)
    square = 0.5 * sharpness * spread(contrast * contrast, group)
    columns = slice(group * GROUP * LANES, (group + 1) * GROUP * LANES)

    def step(i, carry):
        at = pl.ds(pl.multiple_of(i * rows, rows), rows)
        for k in range(rows // 8):
            at = pl.ds(pl.multiple_of(i * rows + k * 8, 8), 8)
            terms = cross[at, columns]
            norm = jnp.concatenate([norms[at, :]] * GROUP, axis=1)
            carry = body(at, columns, twice * terms - square * norm, terms, norm, carry)
        return carry

    return lax.fori_loop(0, cross.shape[0] // rows, step, init, unroll=unroll)


def highest_of(cross, norms, group, contrast):
    low = jnp.full((8, GROUP * LANES), -jnp.inf, jnp.float32)
    high = scan_rows(
        cross, norms, group, contrast, lambda a, b, s, c, n, high: jnp.maximum(high, s), low
    )
    return jnp.max(high, axis=0, keepdims=True)


def own_refit(cross, norms, contrast, prior):
    logs, quotients = [], []
    for group in range(cross.shape[1] // (GROUP * LANES)):
        high = highest_of(cross, norms, group, contrast)
        wide = jnp.broadcast_to(high, (8, GROUP * LANES))

        def body(at, columns, scored, terms, norm, carry):
            total, along, weight = carry
            e = jnp.exp(scored - wide)
            return total + e, along + e * terms, weight + e * norm

        zero = jnp.zeros((8, GROUP * LANES), jnp.float32)
        total, along, weight = (
            jnp.sum(v, axis=0, keepdims=True)
            for v in scan_rows(cross, norms, group, contrast, body, (zero,) * 3)
        )
        first = spread(prior, group)[:1]
        lower = weight + prior_weight * total
        logs.append(high + jnp.log(lower))
        quotients.append((along + prior_weight * first * total) / lower)
    return folded(logs), folded(quotients)


def own_total(cross, norms, contrast):
    logs = []
    for group in range(cross.shape[1] // (GROUP * LANES)):
        high = highest_of(cross, norms, group, contrast)
        wide = jnp.broadcast_to(high, (8, GROUP * LANES))
        total = scan_rows(
            cross,
            norms,
            group,
            contrast,
            lambda a, b, s, c, n, total: total + jnp.exp(s - wide),
            jnp.zeros((8, GROUP * LANES), jnp.float32),
        )
        logs.append(high + jnp.log(jnp.sum(total, axis=0, keepdims=True)))
    return folded(logs)


def combined(received):
    logs, quotients = received[:, :8], received[:, 8:]
    share = jnp.exp(logs - jnp.max(logs, axis=0, keepdims=True))
    return jnp.sum(share * quotients, axis=0) / jnp.sum(share, axis=0)


def combined_log(logs):
    high = jnp.max(logs, axis=0)
    return high + jnp.log(jnp.sum(jnp.exp(logs - high[None]), axis=0))


def send_refit(out, cross, norms, contrast, prior):
    logs, quotients = own_refit(cross, norms, contrast, prior)
    out[...] = jnp.broadcast_to(jnp.concatenate([logs, quotients], axis=0)[None], out.shape)


def squares(held, norms, scale):
    rows = 32

    def step(i, _):
        at = pl.ds(pl.multiple_of(i * rows, rows), rows)
        wide = held[at, :].astype(jnp.float32)
        summed = jnp.sum(wide * wide, axis=1, keepdims=True) * scale
        norms[at, :] = jnp.broadcast_to(summed, (rows, LANES))
        return 0

    lax.fori_loop(0, held.shape[0] // rows, step, 0, unroll=2)


def products(held, images, cross, scale, before=lambda k: None):
    columns = 256
    for k in range(images.shape[0] // columns):
        at = slice(k * columns, (k + 1) * columns)
        before(k)
        product = lax.dot_general(
            held[...], images[at, :], (((1,), (1,)), ((), ())), preferred_element_type=jnp.float32
        )
        cross[:, at] = product if scale is None else product * scale


def first_kernel(images, references, prior, cross, kept, norms, out, held, semaphores):
    columns = 256
    copies = [pltpu.make_async_copy(references, held, semaphores.at[0])]
    for k in range(images.shape[0] // columns):
        at = pl.ds(k * columns, columns)
        copies.append(
            pltpu.make_async_copy(images.at[at], kept.at[at], semaphores.at[k + 1])
        )
    for copy in copies:
        copy.start()
    copies[0].wait()
    squares(held, norms, 1.0)
    products(held, kept, cross, None, lambda k: copies[k + 1].wait())
    send_refit(out, cross, norms, prior[...], prior[...])


def refit_kernel(received, cross, norms, prior, out):
    send_refit(out, cross, norms, combined(received[...]), prior[...])


def total_kernel(received, cross, norms, contrast, out):
    contrast[...] = combined(received[...])
    out[...] = jnp.broadcast_to(own_total(cross, norms, contrast[...])[None], out.shape)


def sum_kernel(received, cross, norms, contrast, images, out, weights):
    log_total = combined_log(received[...])
    for group in range(cross.shape[1] // (GROUP * LANES)):
        wide = spread(log_total, group)
        scale = spread(contrast[...], group)
        columns = slice(group * GROUP * LANES, (group + 1) * GROUP * LANES)
        twice = sharpness * scale
        square = 0.5 * sharpness * (scale * scale)

        def step(i, _):
            at = pl.ds(pl.multiple_of(i * 16, 16), 16)
            parts = []
            for k in range(2):
                part = pl.ds(pl.multiple_of(i * 16 + k * 8, 8), 8)
                norm = jnp.concatenate([norms[part, :]] * GROUP, axis=1)
                scored = twice * cross[part, columns] - square * norm
                parts.append(jnp.exp(scored - wide) * scale)
            weights[at, columns] = jnp.concatenate(parts, axis=0).astype(jnp.bfloat16)
            return 0

        lax.fori_loop(0, cross.shape[0] // 16, step, 0, unroll=4)
    width = 512
    for k in range(images.shape[1] // width):
        at = slice(k * width, (k + 1) * width)
        out[:, at] = jnp.dot(
            weights[...], images[:, at], preferred_element_type=jnp.float32
        ).astype(jnp.bfloat16)


def score_kernel(gathered, images, contrast, out, result, cross, norms, semaphore):
    copy = pltpu.make_async_copy(gathered, result, semaphore)
    copy.start()
    width = gathered.shape[1]
    squares(gathered, norms, 1.0 / width)
    products(gathered, images, cross, width**-0.5)
    out[...] = jnp.broadcast_to(own_total(cross, norms, contrast[...])[None], out.shape)
    copy.wait()


VMEM = pl.BlockSpec(memory_space=pltpu.VMEM)
HBM = pl.BlockSpec(memory_space=pltpu.HBM)


def call(kernel, outs, *args, ins=None, specs=None, scratch=(), limit=16, flops=0):
    return pl.pallas_call(
        kernel,
        out_shape=outs,
        in_specs=ins or [VMEM] * len(args),
        out_specs=specs or (VMEM,) * len(outs),
        scratch_shapes=scratch,
        compiler_params=pltpu.CompilerParams(vmem_limit_bytes=limit * 2**20),
        cost_estimate=pl.CostEstimate(
            flops=flops, bytes_accessed=2**22, transcendentals=2**19
        ),
    )(*args)


def per_device(images, references, initial_contrast):
    count, width = images.shape
    refs = references.shape[0]
    devices = lax.axis_size("ref")
    f32, bf16 = jnp.float32, jnp.bfloat16
    per_image = (count // LANES, LANES)
    prior = initial_contrast.reshape(per_image)
    two = pltpu.VMEM((devices, 2 * per_image[0], LANES), f32)
    one = pltpu.VMEM((devices, *per_image), f32)
    flops = 2 * count * refs * width

    cross, kept, norms, own = call(
        first_kernel,
        (
            pltpu.VMEM((refs, count), f32),
            pltpu.VMEM((count, width), bf16),
            pltpu.VMEM((refs, LANES), f32),
            two,
        ),
        images,
        references,
        prior,
        ins=[HBM, HBM, VMEM],
        scratch=[pltpu.VMEM((refs, width), bf16), pltpu.SemaphoreType.DMA((5,))],
        limit=56,
        flops=flops,
    )
    for _ in range(ITERS - 1):
        (own,) = call(refit_kernel, (two,), exchanged(own, "ref"), cross, norms, prior)
    contrast, own = call(
        total_kernel,
        (pltpu.VMEM(per_image, f32), one),
        exchanged(own, "ref"),
        cross,
        norms,
    )
    (img_partial,) = call(
        sum_kernel,
        (pltpu.VMEM((refs, width), bf16),),
        exchanged(own, "ref"),
        cross,
        norms,
        contrast,
        kept,
        scratch=[pltpu.VMEM((refs, count), bf16)],
        flops=flops,
    )
    gathered = gathered_rows(normalize(summed_share(img_partial)))
    own, new_references = call(
        score_kernel,
        (one, jax.ShapeDtypeStruct((refs, width), bf16)),
        gathered,
        kept,
        contrast,
        specs=(VMEM, HBM),
        scratch=[
            pltpu.VMEM((refs, count), f32),
            pltpu.VMEM((refs, LANES), f32),
            pltpu.SemaphoreType.DMA,
        ],
        flops=flops,
    )
    loglik = combined_log(exchanged(own, "ref")) - math.log(refs * devices)
    return (new_references, contrast.reshape(count), loglik.reshape(count))


def solution(mesh):
    placed = (P("img", None), P("ref", None), P("img"))
    return jax.shard_map(
        per_device,
        mesh=mesh,
        in_specs=placed,
        out_specs=(P("ref", None), P("img"), P("img")),
        check_vma=False,
    )
```

```python
import math

import jax
import jax.numpy as jnp
from jax import lax
from jax.experimental import pallas as pl
from jax.experimental.pallas import tpu as pltpu
from jax.sharding import PartitionSpec as P

ITERS = 3


sharpness = 2.0
prior_weight = 1.0
epsilon = 1e-06

X, Y = 4, 8
NEAR = [[x * Y + 2 * pair + side for x in range(X) for side in range(2)] for pair in range(Y // 2)]
FAR = [[x * Y + 2 * pair + side for pair in range(Y // 2)] for x in range(X) for side in range(2)]


def exchanged(pieces, axis, groups=None):
    return lax.all_to_all(pieces, axis, 0, 0, tiled=True, axis_index_groups=groups)


def sent_to_all(value, axis, groups=None):
    devices = len(groups[0]) if groups else lax.axis_size(axis)
    return exchanged(jnp.broadcast_to(value[None], (devices, *value.shape)), axis, groups)


def summed_share(partial):
    rows, width = partial.shape
    for groups in (NEAR, FAR):
        rows //= len(groups[0])
        pieces = partial.astype(jnp.bfloat16).reshape(len(groups[0]), rows, width)
        partial = jnp.sum(exchanged(pieces, "img", groups).astype(jnp.float32), axis=0)
    return partial


def gathered_rows(share):
    for groups in (FAR, NEAR):
        share = sent_to_all(share, "img", groups).reshape(-1, share.shape[-1])
    return share


def normalize(sums):
    meansq = jnp.mean(sums * sums, axis=1)
    return (sums * lax.rsqrt(meansq + epsilon)[:, None]).astype(jnp.bfloat16)


LANES = 128
BLOCK = 256
ROWS = BLOCK // LANES


def laid_out(value, k):
    return jnp.concatenate([value[k * ROWS + j : k * ROWS + j + 1] for j in range(ROWS)], axis=1)


def folded(parts):
    rows = [part[:, j * LANES : (j + 1) * LANES] for part in parts for j in range(ROWS)]
    return jnp.concatenate(rows, axis=0)


def block_at(k):
    return slice(k * BLOCK, (k + 1) * BLOCK)


def scored(terms, norms, contrast):
    wide = jnp.concatenate([norms[...]] * ROWS, axis=1)
    return sharpness * contrast * terms - 0.5 * sharpness * (contrast * contrast) * wide, wide


def own_refit(terms, norms, contrast, prior):
    scores, wide = scored(terms, norms, contrast)
    high = jnp.max(scores, axis=0, keepdims=True)
    e = jnp.exp(scores - high)
    total = jnp.sum(e, axis=0, keepdims=True)
    upper = jnp.sum(e * terms, axis=0, keepdims=True) + prior_weight * prior * total
    lower = jnp.sum(e * wide, axis=0, keepdims=True) + prior_weight * total
    return high + jnp.log(lower), upper / lower


def own_total(terms, norms, contrast):
    scores, _ = scored(terms, norms, contrast)
    high = jnp.max(scores, axis=0, keepdims=True)
    return high + jnp.log(jnp.sum(jnp.exp(scores - high), axis=0, keepdims=True))


def combined(received):
    logs, quotients = received[:, :8], received[:, 8:]
    share = jnp.exp(logs - jnp.max(logs, axis=0, keepdims=True))
    return jnp.sum(share * quotients, axis=0) / jnp.sum(share, axis=0)


def combined_log(logs):
    high = jnp.max(logs, axis=0)
    return high + jnp.log(jnp.sum(jnp.exp(logs - high[None]), axis=0))


def send(out, *parts):
    own = jnp.concatenate([folded(part) for part in parts], axis=0)
    out[...] = jnp.broadcast_to(own[None], out.shape)


def squares(held, norms, scale):
    rows = 64
    for i in range(held.shape[0] // rows):
        at = slice(i * rows, (i + 1) * rows)
        summed = jnp.zeros((rows, LANES), jnp.float32)
        for k in range(held.shape[1] // LANES):
            wide = held[at, k * LANES : (k + 1) * LANES].astype(jnp.float32)
            summed = summed + wide * wide
        norm = jnp.sum(summed, axis=1, keepdims=True) * scale
        norms[at, :] = jnp.broadcast_to(norm, (rows, LANES))


def product(held, images, k):
    return lax.dot_general(
        held[...], images[block_at(k), :], (((1,), (1,)), ((), ())), preferred_element_type=jnp.float32
    )


def first_kernel(images, references, prior, cross, kept, norms, out, held, semaphores):
    halves = 2
    size = images.shape[0] // halves
    copies = [pltpu.make_async_copy(references, held, semaphores.at[halves])]
    for h in range(halves):
        at = pl.ds(h * size, size)
        copies.append(pltpu.make_async_copy(images.at[at], kept.at[at], semaphores.at[h]))
    for copy in copies:
        copy.start()
    copies[0].wait()
    logs, quotients = [], []
    for h in range(halves):
        copies[h + 1].wait()
        if h == 0:
            squares(held, norms, 1.0)
        blocks = range(h * size // BLOCK, (h + 1) * size // BLOCK)
        for k in blocks:
            cross[:, block_at(k)] = product(held, kept, k)
        for k in blocks:
            start = laid_out(prior, k)
            log, quotient = own_refit(cross[:, block_at(k)], norms, start, start)
            logs.append(log)
            quotients.append(quotient)
    send(out, logs, quotients)


def refit_kernel(received, cross, norms, prior, images, out):
    contrast = combined(received[...])
    logs, quotients = [], []
    for k in range(cross.shape[1] // BLOCK):
        log, quotient = own_refit(
            cross[:, block_at(k)], norms, laid_out(contrast, k), laid_out(prior, k)
        )
        logs.append(log)
        quotients.append(quotient)
    send(out, logs, quotients)


def total_kernel(received, cross, norms, images, contrast, out):
    found = combined(received[...])
    contrast[...] = found
    send(
        out,
        [
            own_total(cross[:, block_at(k)], norms, laid_out(found, k))
            for k in range(cross.shape[1] // BLOCK)
        ],
    )


def sum_kernel(received, cross, norms, contrast, images, out, weights):
    log_total = combined_log(received[...])
    for k in range(cross.shape[1] // BLOCK):
        scale = laid_out(contrast, k)
        scores, _ = scored(cross[:, block_at(k)], norms, scale)
        posterior = jnp.exp(scores - laid_out(log_total, k))
        weights[:, block_at(k)] = (posterior * scale).astype(jnp.bfloat16)
    width = 512
    for k in range(images.shape[1] // width):
        at = slice(k * width, (k + 1) * width)
        out[:, at] = jnp.dot(
            weights[...], images[:, at], preferred_element_type=jnp.float32
        ).astype(jnp.bfloat16)


def score_kernel(gathered, images, contrast, out, result, norms, semaphore):
    copy = pltpu.make_async_copy(gathered, result, semaphore)
    copy.start()
    width = gathered.shape[1]
    squares(gathered, norms, 1.0 / width)
    logs = []
    for k in range(images.shape[0] // BLOCK):
        terms = product(gathered, images, k) * width**-0.5
        logs.append(own_total(terms, norms, laid_out(contrast, k)))
    send(out, logs)
    copy.wait()


VMEM = pl.BlockSpec(memory_space=pltpu.VMEM)
HBM = pl.BlockSpec(memory_space=pltpu.HBM)


def call(kernel, outs, *args, ins=None, specs=None, scratch=(), limit=16, flops=0):
    return pl.pallas_call(
        kernel,
        out_shape=outs,
        in_specs=ins or [VMEM] * len(args),
        out_specs=specs or (VMEM,) * len(outs),
        scratch_shapes=scratch,
        compiler_params=pltpu.CompilerParams(vmem_limit_bytes=limit * 2**20),
        cost_estimate=pl.CostEstimate(
            flops=flops, bytes_accessed=2**22, transcendentals=2**19
        ),
    )(*args)


def per_device(images, references, initial_contrast):
    count, width = images.shape
    refs = references.shape[0]
    devices = lax.axis_size("ref")
    f32, bf16 = jnp.float32, jnp.bfloat16
    per_image = (count // LANES, LANES)
    prior = initial_contrast.reshape(per_image)
    two = pltpu.VMEM((devices, 2 * per_image[0], LANES), f32)
    one = pltpu.VMEM((devices, *per_image), f32)
    flops = 2 * count * refs * width

    cross, kept, norms, own = call(
        first_kernel,
        (
            pltpu.VMEM((refs, count), f32),
            pltpu.VMEM((count, width), bf16),
            pltpu.VMEM((refs, LANES), f32),
            two,
        ),
        images,
        references,
        prior,
        ins=[HBM, HBM, VMEM],
        scratch=[pltpu.VMEM((refs, width), bf16), pltpu.SemaphoreType.DMA((3,))],
        limit=54,
        flops=flops,
    )
    for _ in range(ITERS - 1):
        (own,) = call(refit_kernel, (two,), exchanged(own, "ref"), cross, norms, prior, kept)
    contrast, own = call(
        total_kernel,
        (pltpu.VMEM(per_image, f32), one),
        exchanged(own, "ref"),
        cross,
        norms,
        kept,
    )
    (img_partial,) = call(
        sum_kernel,
        (pltpu.VMEM((refs, width), bf16),),
        exchanged(own, "ref"),
        cross,
        norms,
        contrast,
        kept,
        scratch=[pltpu.VMEM((refs, count), bf16)],
        flops=flops,
    )
    gathered = gathered_rows(normalize(summed_share(img_partial)))
    own, new_references = call(
        score_kernel,
        (one, jax.ShapeDtypeStruct((refs, width), bf16)),
        gathered,
        kept,
        contrast,
        specs=(VMEM, HBM),
        scratch=[
            pltpu.VMEM((refs, LANES), f32),
            pltpu.SemaphoreType.DMA,
        ],
        flops=flops,
    )
    loglik = combined_log(exchanged(own, "ref")) - math.log(refs * devices)
    return (new_references, contrast.reshape(count), loglik.reshape(count))


def solution(mesh):
    placed = (P("img", None), P("ref", None), P("img"))
    return jax.shard_map(
        per_device,
        mesh=mesh,
        in_specs=placed,
        out_specs=(P("ref", None), P("img"), P("img")),
        check_vma=False,
    )
```

```python
import math

import jax
import jax.numpy as jnp
from jax import lax
from jax.experimental import pallas as pl
from jax.experimental.pallas import tpu as pltpu
from jax.sharding import PartitionSpec as P

ITERS = 3


sharpness = 2.0
prior_weight = 1.0
epsilon = 1e-06

X, Y, Z, CORES = 4, 8, 8, 2
PLANE = ("img", "ref")


def device(x, y, ref):
    return ((x % X) * Y + y % Y) * Z * CORES + ref


SIDES = [(a, b) for a in range(2) for b in range(2)]
PLACES = [(2 * i, 2 * j) for i in range(X // 2) for j in range(Y // 2)]
CORNERS = [(ref, ref % CORES) for ref in range(Z * CORES)]
BLOCKS = [
    [device(x + a + core, y + b + core, ref) for a, b in SIDES]
    for ref, core in CORNERS
    for x, y in PLACES
]
SPREAD = [
    [device(x + a + core, y + b + core, ref) for x, y in PLACES]
    for ref, core in CORNERS
    for a, b in SIDES
]


def exchanged(pieces, axis, groups=None):
    return lax.all_to_all(pieces, axis, 0, 0, tiled=True, axis_index_groups=groups)


def sent_to_all(value, axis, groups):
    return exchanged(jnp.broadcast_to(value[None], (len(groups[0]), *value.shape)), axis, groups)


def summed_share(partial):
    rows, width = partial.shape
    for groups in (BLOCKS, SPREAD):
        rows //= len(groups[0])
        pieces = partial.astype(jnp.bfloat16).reshape(len(groups[0]), rows, width)
        partial = jnp.sum(exchanged(pieces, PLANE, groups).astype(jnp.float32), axis=0)
    return partial


def gathered_rows(share):
    for groups in (SPREAD, BLOCKS):
        share = sent_to_all(share, PLANE, groups).reshape(-1, share.shape[-1])
    return share


def normalize(sums):
    meansq = jnp.mean(sums * sums, axis=1)
    return (sums * lax.rsqrt(meansq + epsilon)[:, None]).astype(jnp.bfloat16)


LANES = 128
BLOCK = 256
ROWS = BLOCK // LANES


def laid_out(value, k):
    return jnp.concatenate([value[k * ROWS + j : k * ROWS + j + 1] for j in range(ROWS)], axis=1)


def folded(parts):
    rows = [part[:, j * LANES : (j + 1) * LANES] for part in parts for j in range(ROWS)]
    return jnp.concatenate(rows, axis=0)


def block_at(k):
    return slice(k * BLOCK, (k + 1) * BLOCK)


def scored(terms, norms, contrast):
    wide = jnp.concatenate([norms[...]] * ROWS, axis=1)
    return sharpness * contrast * terms - 0.5 * sharpness * (contrast * contrast) * wide, wide


def own_refit(terms, norms, contrast, prior):
    scores, wide = scored(terms, norms, contrast)
    high = jnp.max(scores, axis=0, keepdims=True)
    e = jnp.exp(scores - high)
    total = jnp.sum(e, axis=0, keepdims=True)
    upper = jnp.sum(e * terms, axis=0, keepdims=True) + prior_weight * prior * total
    lower = jnp.sum(e * wide, axis=0, keepdims=True) + prior_weight * total
    return high + jnp.log(lower), upper / lower


def own_total(terms, norms, contrast):
    scores, _ = scored(terms, norms, contrast)
    high = jnp.max(scores, axis=0, keepdims=True)
    return high + jnp.log(jnp.sum(jnp.exp(scores - high), axis=0, keepdims=True))


def combined(received):
    logs, quotients = received[:, :8], received[:, 8:]
    share = jnp.exp(logs - jnp.max(logs, axis=0, keepdims=True))
    return jnp.sum(share * quotients, axis=0) / jnp.sum(share, axis=0)


def combined_log(logs):
    high = jnp.max(logs, axis=0)
    return high + jnp.log(jnp.sum(jnp.exp(logs - high[None]), axis=0))


def send(out, *parts):
    own = jnp.concatenate([folded(part) for part in parts], axis=0)
    out[...] = jnp.broadcast_to(own[None], out.shape)


def squares(held, norms, scale):
    rows = 64
    for i in range(held.shape[0] // rows):
        at = slice(i * rows, (i + 1) * rows)
        summed = jnp.zeros((rows, LANES), jnp.float32)
        for k in range(held.shape[1] // LANES):
            wide = held[at, k * LANES : (k + 1) * LANES].astype(jnp.float32)
            summed = summed + wide * wide
        norm = jnp.sum(summed, axis=1, keepdims=True) * scale
        norms[at, :] = jnp.broadcast_to(norm, (rows, LANES))


def product(held, images, k):
    return lax.dot_general(
        held[...], images[block_at(k), :], (((1,), (1,)), ((), ())), preferred_element_type=jnp.float32
    )


def first_kernel(images, references, prior, cross, kept, norms, out, held, semaphores):
    halves = 2
    size = images.shape[0] // halves
    copies = [pltpu.make_async_copy(references, held, semaphores.at[halves])]
    for h in range(halves):
        at = pl.ds(h * size, size)
        copies.append(pltpu.make_async_copy(images.at[at], kept.at[at], semaphores.at[h]))
    for copy in copies:
        copy.start()
    copies[0].wait()
    logs, quotients = [], []
    for h in range(halves):
        copies[h + 1].wait()
        if h == 0:
            squares(held, norms, 1.0)
        blocks = range(h * size // BLOCK, (h + 1) * size // BLOCK)
        for k in blocks:
            cross[:, block_at(k)] = product(held, kept, k)
        for k in blocks:
            start = laid_out(prior, k)
            log, quotient = own_refit(cross[:, block_at(k)], norms, start, start)
            logs.append(log)
            quotients.append(quotient)
    send(out, logs, quotients)


def refit_kernel(received, cross, norms, prior, images, out):
    contrast = combined(received[...])
    logs, quotients = [], []
    for k in range(cross.shape[1] // BLOCK):
        log, quotient = own_refit(
            cross[:, block_at(k)], norms, laid_out(contrast, k), laid_out(prior, k)
        )
        logs.append(log)
        quotients.append(quotient)
    send(out, logs, quotients)


def total_kernel(received, cross, norms, images, contrast, out):
    found = combined(received[...])
    contrast[...] = found
    send(
        out,
        [
            own_total(cross[:, block_at(k)], norms, laid_out(found, k))
            for k in range(cross.shape[1] // BLOCK)
        ],
    )


def sum_kernel(received, cross, norms, contrast, images, out, weights):
    log_total = combined_log(received[...])
    for k in range(cross.shape[1] // BLOCK):
        scale = laid_out(contrast, k)
        scores, _ = scored(cross[:, block_at(k)], norms, scale)
        posterior = jnp.exp(scores - laid_out(log_total, k))
        weights[:, block_at(k)] = (posterior * scale).astype(jnp.bfloat16)
    width = 512
    for k in range(images.shape[1] // width):
        at = slice(k * width, (k + 1) * width)
        out[:, at] = jnp.dot(
            weights[...], images[:, at], preferred_element_type=jnp.float32
        ).astype(jnp.bfloat16)


def score_kernel(gathered, images, contrast, out, result, norms, semaphore):
    copy = pltpu.make_async_copy(gathered, result, semaphore)
    copy.start()
    width = gathered.shape[1]
    squares(gathered, norms, 1.0 / width)
    logs = []
    for k in range(images.shape[0] // BLOCK):
        terms = product(gathered, images, k) * width**-0.5
        logs.append(own_total(terms, norms, laid_out(contrast, k)))
    send(out, logs)
    copy.wait()


VMEM = pl.BlockSpec(memory_space=pltpu.VMEM)
HBM = pl.BlockSpec(memory_space=pltpu.HBM)


def call(kernel, outs, *args, ins=None, specs=None, scratch=(), limit=16, flops=0):
    return pl.pallas_call(
        kernel,
        out_shape=outs,
        in_specs=ins or [VMEM] * len(args),
        out_specs=specs or (VMEM,) * len(outs),
        scratch_shapes=scratch,
        compiler_params=pltpu.CompilerParams(vmem_limit_bytes=limit * 2**20),
        cost_estimate=pl.CostEstimate(
            flops=flops, bytes_accessed=2**22, transcendentals=2**19
        ),
    )(*args)


def per_device(images, references, initial_contrast):
    count, width = images.shape
    refs = references.shape[0]
    devices = lax.axis_size("ref")
    f32, bf16 = jnp.float32, jnp.bfloat16
    per_image = (count // LANES, LANES)
    prior = initial_contrast.reshape(per_image)
    two = pltpu.VMEM((devices, 2 * per_image[0], LANES), f32)
    one = pltpu.VMEM((devices, *per_image), f32)
    flops = 2 * count * refs * width

    cross, kept, norms, own = call(
        first_kernel,
        (
            pltpu.VMEM((refs, count), f32),
            pltpu.VMEM((count, width), bf16),
            pltpu.VMEM((refs, LANES), f32),
            two,
        ),
        images,
        references,
        prior,
        ins=[HBM, HBM, VMEM],
        scratch=[pltpu.VMEM((refs, width), bf16), pltpu.SemaphoreType.DMA((3,))],
        limit=54,
        flops=flops,
    )
    for _ in range(ITERS - 1):
        (own,) = call(refit_kernel, (two,), exchanged(own, "ref"), cross, norms, prior, kept)
    contrast, own = call(
        total_kernel,
        (pltpu.VMEM(per_image, f32), one),
        exchanged(own, "ref"),
        cross,
        norms,
        kept,
    )
    (img_partial,) = call(
        sum_kernel,
        (pltpu.VMEM((refs, width), bf16),),
        exchanged(own, "ref"),
        cross,
        norms,
        contrast,
        kept,
        scratch=[pltpu.VMEM((refs, count), bf16)],
        flops=flops,
    )
    gathered = gathered_rows(normalize(summed_share(img_partial)))
    own, new_references = call(
        score_kernel,
        (one, jax.ShapeDtypeStruct((refs, width), bf16)),
        gathered,
        kept,
        contrast,
        specs=(VMEM, HBM),
        scratch=[
            pltpu.VMEM((refs, LANES), f32),
            pltpu.SemaphoreType.DMA,
        ],
        flops=flops,
    )
    loglik = combined_log(exchanged(own, "ref")) - math.log(refs * devices)
    return (new_references, contrast.reshape(count), loglik.reshape(count))


def solution(mesh):
    placed = (P("img", None), P("ref", None), P("img"))
    return jax.shard_map(
        per_device,
        mesh=mesh,
        in_specs=placed,
        out_specs=(P("ref", None), P("img"), P("img")),
        check_vma=False,
    )
```

```python
import math

import jax
import jax.numpy as jnp
from jax import lax
from jax.experimental import pallas as pl
from jax.experimental.pallas import tpu as pltpu
from jax.sharding import PartitionSpec as P

ITERS = 3


sharpness = 2.0
prior_weight = 1.0
epsilon = 1e-06

X, Y, Z, CORES = 4, 8, 8, 2
PLANE = ("img", "ref")


def device(x, y, ref):
    return ((x % X) * Y + y % Y) * Z * CORES + ref


SIDES = [(a, b) for a in range(2) for b in range(2)]
ALONG_X = [2 * i for i in range(X // 2)]
ALONG_Y = [2 * j for j in range(Y // 2)]
CORNERS = [(ref, ref % CORES) for ref in range(Z * CORES)]


def at(ref, core, side, x, y):
    return device(x + side[0] + core, y + side[1] + core, ref)


BLOCKS = [
    [at(*corner, side, x, y) for side in SIDES]
    for corner in CORNERS
    for x in ALONG_X
    for y in ALONG_Y
]
SPREAD = [
    [at(*corner, side, x, y) for x in ALONG_X for y in ALONG_Y]
    for corner in CORNERS
    for side in SIDES
]
FAR = [
    [at(*corner, side, x, y) for y in ALONG_Y]
    for corner in CORNERS
    for side in SIDES
    for x in ALONG_X
]
NEAR = [
    [at(*corner, side, x, y) for side in SIDES for x in ALONG_X]
    for corner in CORNERS
    for y in ALONG_Y
]


def exchanged(pieces, axis, groups=None):
    return lax.all_to_all(pieces, axis, 0, 0, tiled=True, axis_index_groups=groups)


def sent_to_all(value, axis, groups):
    return exchanged(jnp.broadcast_to(value[None], (len(groups[0]), *value.shape)), axis, groups)


def summed_share(partial):
    rows, width = partial.shape
    for groups in (BLOCKS, SPREAD):
        rows //= len(groups[0])
        pieces = partial.astype(jnp.bfloat16).reshape(len(groups[0]), rows, width)
        partial = jnp.sum(exchanged(pieces, PLANE, groups).astype(jnp.float32), axis=0)
    return partial


def gathered_rows(share):
    for groups in (FAR, NEAR):
        share = sent_to_all(share, PLANE, groups).reshape(-1, share.shape[-1])
    return share


def normalize(sums):
    meansq = jnp.mean(sums * sums, axis=1)
    return (sums * lax.rsqrt(meansq + epsilon)[:, None]).astype(jnp.bfloat16)


LANES = 128
BLOCK = 256
ROWS = BLOCK // LANES


def laid_out(value, k):
    return jnp.concatenate([value[k * ROWS + j : k * ROWS + j + 1] for j in range(ROWS)], axis=1)


def folded(parts):
    rows = [part[:, j * LANES : (j + 1) * LANES] for part in parts for j in range(ROWS)]
    return jnp.concatenate(rows, axis=0)


def block_at(k):
    return slice(k * BLOCK, (k + 1) * BLOCK)


def scored(terms, norms, contrast):
    wide = jnp.concatenate([norms[...]] * ROWS, axis=1)
    return sharpness * contrast * terms - 0.5 * sharpness * (contrast * contrast) * wide, wide


def own_refit(terms, norms, contrast, prior):
    scores, wide = scored(terms, norms, contrast)
    high = jnp.max(scores, axis=0, keepdims=True)
    e = jnp.exp(scores - high)
    total = jnp.sum(e, axis=0, keepdims=True)
    upper = jnp.sum(e * terms, axis=0, keepdims=True) + prior_weight * prior * total
    lower = jnp.sum(e * wide, axis=0, keepdims=True) + prior_weight * total
    return high + jnp.log(lower), upper / lower


def own_total(terms, norms, contrast):
    scores, _ = scored(terms, norms, contrast)
    high = jnp.max(scores, axis=0, keepdims=True)
    return high + jnp.log(jnp.sum(jnp.exp(scores - high), axis=0, keepdims=True))


def combined(received):
    logs, quotients = received[:, :8], received[:, 8:]
    share = jnp.exp(logs - jnp.max(logs, axis=0, keepdims=True))
    return jnp.sum(share * quotients, axis=0) / jnp.sum(share, axis=0)


def combined_log(logs):
    high = jnp.max(logs, axis=0)
    return high + jnp.log(jnp.sum(jnp.exp(logs - high[None]), axis=0))


def send(out, *parts):
    own = jnp.concatenate([folded(part) for part in parts], axis=0)
    out[...] = jnp.broadcast_to(own[None], out.shape)


def squares(held, norms, scale):
    rows = 64
    for i in range(held.shape[0] // rows):
        at = slice(i * rows, (i + 1) * rows)
        summed = jnp.zeros((rows, LANES), jnp.float32)
        for k in range(held.shape[1] // LANES):
            wide = held[at, k * LANES : (k + 1) * LANES].astype(jnp.float32)
            summed = summed + wide * wide
        norm = jnp.sum(summed, axis=1, keepdims=True) * scale
        norms[at, :] = jnp.broadcast_to(norm, (rows, LANES))


def product(held, images, k):
    return lax.dot_general(
        held[...], images[block_at(k), :], (((1,), (1,)), ((), ())), preferred_element_type=jnp.float32
    )


def first_kernel(images, references, prior, cross, kept, norms, out, held, semaphores):
    halves = 2
    size = images.shape[0] // halves
    copies = [pltpu.make_async_copy(references, held, semaphores.at[halves])]
    for h in range(halves):
        at = pl.ds(h * size, size)
        copies.append(pltpu.make_async_copy(images.at[at], kept.at[at], semaphores.at[h]))
    for copy in copies:
        copy.start()
    copies[0].wait()
    logs, quotients = [], []
    for h in range(halves):
        copies[h + 1].wait()
        if h == 0:
            squares(held, norms, 1.0)
        blocks = range(h * size // BLOCK, (h + 1) * size // BLOCK)
        for k in blocks:
            cross[:, block_at(k)] = product(held, kept, k)
        for k in blocks:
            start = laid_out(prior, k)
            log, quotient = own_refit(cross[:, block_at(k)], norms, start, start)
            logs.append(log)
            quotients.append(quotient)
    send(out, logs, quotients)


def refit_kernel(received, cross, norms, prior, images, out):
    contrast = combined(received[...])
    logs, quotients = [], []
    for k in range(cross.shape[1] // BLOCK):
        log, quotient = own_refit(
            cross[:, block_at(k)], norms, laid_out(contrast, k), laid_out(prior, k)
        )
        logs.append(log)
        quotients.append(quotient)
    send(out, logs, quotients)


def total_kernel(received, cross, norms, images, contrast, out):
    found = combined(received[...])
    contrast[...] = found
    send(
        out,
        [
            own_total(cross[:, block_at(k)], norms, laid_out(found, k))
            for k in range(cross.shape[1] // BLOCK)
        ],
    )


def sum_kernel(received, cross, norms, contrast, images, out, weights):
    log_total = combined_log(received[...])
    for k in range(cross.shape[1] // BLOCK):
        scale = laid_out(contrast, k)
        scores, _ = scored(cross[:, block_at(k)], norms, scale)
        posterior = jnp.exp(scores - laid_out(log_total, k))
        weights[:, block_at(k)] = (posterior * scale).astype(jnp.bfloat16)
    width = 512
    for k in range(images.shape[1] // width):
        at = slice(k * width, (k + 1) * width)
        out[:, at] = jnp.dot(
            weights[...], images[:, at], preferred_element_type=jnp.float32
        ).astype(jnp.bfloat16)


def score_kernel(gathered, images, contrast, out, result, norms, semaphore):
    copy = pltpu.make_async_copy(gathered, result, semaphore)
    copy.start()
    width = gathered.shape[1]
    squares(gathered, norms, 1.0 / width)
    logs = []
    for k in range(images.shape[0] // BLOCK):
        terms = product(gathered, images, k) * width**-0.5
        logs.append(own_total(terms, norms, laid_out(contrast, k)))
    send(out, logs)
    copy.wait()


VMEM = pl.BlockSpec(memory_space=pltpu.VMEM)
HBM = pl.BlockSpec(memory_space=pltpu.HBM)


def call(kernel, outs, *args, ins=None, specs=None, scratch=(), limit=16, flops=0):
    return pl.pallas_call(
        kernel,
        out_shape=outs,
        in_specs=ins or [VMEM] * len(args),
        out_specs=specs or (VMEM,) * len(outs),
        scratch_shapes=scratch,
        compiler_params=pltpu.CompilerParams(vmem_limit_bytes=limit * 2**20),
        cost_estimate=pl.CostEstimate(
            flops=flops, bytes_accessed=2**22, transcendentals=2**19
        ),
    )(*args)


def per_device(images, references, initial_contrast):
    count, width = images.shape
    refs = references.shape[0]
    devices = lax.axis_size("ref")
    f32, bf16 = jnp.float32, jnp.bfloat16
    per_image = (count // LANES, LANES)
    prior = initial_contrast.reshape(per_image)
    two = pltpu.VMEM((devices, 2 * per_image[0], LANES), f32)
    one = pltpu.VMEM((devices, *per_image), f32)
    flops = 2 * count * refs * width

    cross, kept, norms, own = call(
        first_kernel,
        (
            pltpu.VMEM((refs, count), f32),
            pltpu.VMEM((count, width), bf16),
            pltpu.VMEM((refs, LANES), f32),
            two,
        ),
        images,
        references,
        prior,
        ins=[HBM, HBM, VMEM],
        scratch=[pltpu.VMEM((refs, width), bf16), pltpu.SemaphoreType.DMA((3,))],
        limit=54,
        flops=flops,
    )
    for _ in range(ITERS - 1):
        (own,) = call(refit_kernel, (two,), exchanged(own, "ref"), cross, norms, prior, kept)
    contrast, own = call(
        total_kernel,
        (pltpu.VMEM(per_image, f32), one),
        exchanged(own, "ref"),
        cross,
        norms,
        kept,
    )
    (img_partial,) = call(
        sum_kernel,
        (pltpu.VMEM((refs, width), bf16),),
        exchanged(own, "ref"),
        cross,
        norms,
        contrast,
        kept,
        scratch=[pltpu.VMEM((refs, count), bf16)],
        flops=flops,
    )
    gathered = gathered_rows(normalize(summed_share(img_partial)))
    own, new_references = call(
        score_kernel,
        (one, jax.ShapeDtypeStruct((refs, width), bf16)),
        gathered,
        kept,
        contrast,
        specs=(VMEM, HBM),
        scratch=[
            pltpu.VMEM((refs, LANES), f32),
            pltpu.SemaphoreType.DMA,
        ],
        flops=flops,
    )
    loglik = combined_log(exchanged(own, "ref")) - math.log(refs * devices)
    return (new_references, contrast.reshape(count), loglik.reshape(count))


def solution(mesh):
    placed = (P("img", None), P("ref", None), P("img"))
    return jax.shard_map(
        per_device,
        mesh=mesh,
        in_specs=placed,
        out_specs=(P("ref", None), P("img"), P("img")),
        check_vma=False,
    )
```

```python
import math

import jax
import jax.numpy as jnp
from jax import lax
from jax.experimental import pallas as pl
from jax.experimental.pallas import tpu as pltpu
from jax.sharding import PartitionSpec as P

ITERS = 3


sharpness = 2.0
prior_weight = 1.0
epsilon = 1e-06

X, Y, Z, CORES = 4, 8, 8, 2
PLANE = ("img", "ref")


def device(x, y, ref):
    return ((x % X) * Y + y % Y) * Z * CORES + ref


SIDES = [(a, b) for a in range(2) for b in range(2)]
REFS = range(Z * CORES)
BLOCKS = [
    [device(2 * i + a + ref % CORES, 2 * j + b + ref % CORES, ref) for a, b in SIDES]
    for ref in REFS
    for i in range(X // 2)
    for j in range(Y // 2)
]
ORDER = [(k % 2, (k // 2 + k % 2 * 2) % 4) for k in range(X * Y // 4)]
SPREAD = [[device(2 * i + a, 2 * j + b, ref) for i, j in ORDER] for ref in REFS for a, b in SIDES]


def exchanged(pieces, axis, groups=None):
    return lax.all_to_all(pieces, axis, 0, 0, tiled=True, axis_index_groups=groups)


def sent_to_all(value, axis, groups):
    return exchanged(jnp.broadcast_to(value[None], (len(groups[0]), *value.shape)), axis, groups)


def summed_share(partial):
    rows, width = partial.shape
    for groups in (BLOCKS, SPREAD):
        rows //= len(groups[0])
        pieces = partial.astype(jnp.bfloat16).reshape(len(groups[0]), rows, width)
        partial = jnp.sum(exchanged(pieces, PLANE, groups).astype(jnp.float32), axis=0)
    return partial


def gathered_rows(share):
    for groups in (SPREAD, BLOCKS):
        share = sent_to_all(share, PLANE, groups).reshape(-1, share.shape[-1])
    return share


def normalize(sums):
    meansq = jnp.mean(sums * sums, axis=1)
    return (sums * lax.rsqrt(meansq + epsilon)[:, None]).astype(jnp.bfloat16)


LANES = 128
BLOCK = 256
ROWS = BLOCK // LANES


def laid_out(value, k):
    return jnp.concatenate([value[k * ROWS + j : k * ROWS + j + 1] for j in range(ROWS)], axis=1)


def folded(parts):
    rows = [part[:, j * LANES : (j + 1) * LANES] for part in parts for j in range(ROWS)]
    return jnp.concatenate(rows, axis=0)


def block_at(k):
    return slice(k * BLOCK, (k + 1) * BLOCK)


def scored(terms, norms, contrast):
    wide = jnp.concatenate([norms[...]] * ROWS, axis=1)
    return sharpness * contrast * terms - 0.5 * sharpness * (contrast * contrast) * wide, wide


def own_refit(terms, norms, contrast, prior):
    scores, wide = scored(terms, norms, contrast)
    high = jnp.max(scores, axis=0, keepdims=True)
    e = jnp.exp(scores - high)
    total = jnp.sum(e, axis=0, keepdims=True)
    upper = jnp.sum(e * terms, axis=0, keepdims=True) + prior_weight * prior * total
    lower = jnp.sum(e * wide, axis=0, keepdims=True) + prior_weight * total
    return high + jnp.log(lower), upper / lower


def own_total(terms, norms, contrast):
    scores, _ = scored(terms, norms, contrast)
    high = jnp.max(scores, axis=0, keepdims=True)
    return high + jnp.log(jnp.sum(jnp.exp(scores - high), axis=0, keepdims=True))


def combined(received):
    logs, quotients = received[:, :8], received[:, 8:]
    share = jnp.exp(logs - jnp.max(logs, axis=0, keepdims=True))
    return jnp.sum(share * quotients, axis=0) / jnp.sum(share, axis=0)


def combined_log(logs):
    high = jnp.max(logs, axis=0)
    return high + jnp.log(jnp.sum(jnp.exp(logs - high[None]), axis=0))


def send(out, *parts):
    own = jnp.concatenate([folded(part) for part in parts], axis=0)
    out[...] = jnp.broadcast_to(own[None], out.shape)


def squares(held, norms, scale):
    rows = 64
    for i in range(held.shape[0] // rows):
        at = slice(i * rows, (i + 1) * rows)
        summed = jnp.zeros((rows, LANES), jnp.float32)
        for k in range(held.shape[1] // LANES):
            wide = held[at, k * LANES : (k + 1) * LANES].astype(jnp.float32)
            summed = summed + wide * wide
        norm = jnp.sum(summed, axis=1, keepdims=True) * scale
        norms[at, :] = jnp.broadcast_to(norm, (rows, LANES))


def product(held, images, k):
    return lax.dot_general(
        held[...], images[block_at(k), :], (((1,), (1,)), ((), ())), preferred_element_type=jnp.float32
    )


def first_kernel(images, references, prior, cross, kept, norms, out, held, semaphores):
    halves = 2
    size = images.shape[0] // halves
    copies = [pltpu.make_async_copy(references, held, semaphores.at[halves])]
    for h in range(halves):
        at = pl.ds(h * size, size)
        copies.append(pltpu.make_async_copy(images.at[at], kept.at[at], semaphores.at[h]))
    for copy in copies:
        copy.start()
    copies[0].wait()
    logs, quotients = [], []
    for h in range(halves):
        copies[h + 1].wait()
        if h == 0:
            squares(held, norms, 1.0)
        blocks = range(h * size // BLOCK, (h + 1) * size // BLOCK)
        for k in blocks:
            cross[:, block_at(k)] = product(held, kept, k)
        for k in blocks:
            start = laid_out(prior, k)
            log, quotient = own_refit(cross[:, block_at(k)], norms, start, start)
            logs.append(log)
            quotients.append(quotient)
    send(out, logs, quotients)


def refit_kernel(received, cross, norms, prior, images, out):
    contrast = combined(received[...])
    logs, quotients = [], []
    for k in range(cross.shape[1] // BLOCK):
        log, quotient = own_refit(
            cross[:, block_at(k)], norms, laid_out(contrast, k), laid_out(prior, k)
        )
        logs.append(log)
        quotients.append(quotient)
    send(out, logs, quotients)


def total_kernel(received, cross, norms, images, contrast, out):
    found = combined(received[...])
    contrast[...] = found
    send(
        out,
        [
            own_total(cross[:, block_at(k)], norms, laid_out(found, k))
            for k in range(cross.shape[1] // BLOCK)
        ],
    )


def sum_kernel(received, cross, norms, contrast, images, out, weights):
    log_total = combined_log(received[...])
    for k in range(cross.shape[1] // BLOCK):
        scale = laid_out(contrast, k)
        scores, _ = scored(cross[:, block_at(k)], norms, scale)
        posterior = jnp.exp(scores - laid_out(log_total, k))
        weights[:, block_at(k)] = (posterior * scale).astype(jnp.bfloat16)
    width = 512
    for k in range(images.shape[1] // width):
        at = slice(k * width, (k + 1) * width)
        out[:, at] = jnp.dot(
            weights[...], images[:, at], preferred_element_type=jnp.float32
        ).astype(jnp.bfloat16)


def score_kernel(gathered, images, contrast, out, result, norms, semaphore):
    copy = pltpu.make_async_copy(gathered, result, semaphore)
    copy.start()
    width = gathered.shape[1]
    squares(gathered, norms, 1.0 / width)
    logs = []
    for k in range(images.shape[0] // BLOCK):
        terms = product(gathered, images, k) * width**-0.5
        logs.append(own_total(terms, norms, laid_out(contrast, k)))
    send(out, logs)
    copy.wait()


VMEM = pl.BlockSpec(memory_space=pltpu.VMEM)
HBM = pl.BlockSpec(memory_space=pltpu.HBM)


def call(kernel, outs, *args, ins=None, specs=None, scratch=(), limit=16, flops=0):
    return pl.pallas_call(
        kernel,
        out_shape=outs,
        in_specs=ins or [VMEM] * len(args),
        out_specs=specs or (VMEM,) * len(outs),
        scratch_shapes=scratch,
        compiler_params=pltpu.CompilerParams(vmem_limit_bytes=limit * 2**20),
        cost_estimate=pl.CostEstimate(
            flops=flops, bytes_accessed=2**22, transcendentals=2**19
        ),
    )(*args)


def per_device(images, references, initial_contrast):
    count, width = images.shape
    refs = references.shape[0]
    devices = lax.axis_size("ref")
    f32, bf16 = jnp.float32, jnp.bfloat16
    per_image = (count // LANES, LANES)
    prior = initial_contrast.reshape(per_image)
    two = pltpu.VMEM((devices, 2 * per_image[0], LANES), f32)
    one = pltpu.VMEM((devices, *per_image), f32)
    flops = 2 * count * refs * width

    cross, kept, norms, own = call(
        first_kernel,
        (
            pltpu.VMEM((refs, count), f32),
            pltpu.VMEM((count, width), bf16),
            pltpu.VMEM((refs, LANES), f32),
            two,
        ),
        images,
        references,
        prior,
        ins=[HBM, HBM, VMEM],
        scratch=[pltpu.VMEM((refs, width), bf16), pltpu.SemaphoreType.DMA((3,))],
        limit=54,
        flops=flops,
    )
    for _ in range(ITERS - 1):
        (own,) = call(refit_kernel, (two,), exchanged(own, "ref"), cross, norms, prior, kept)
    contrast, own = call(
        total_kernel,
        (pltpu.VMEM(per_image, f32), one),
        exchanged(own, "ref"),
        cross,
        norms,
        kept,
    )
    (img_partial,) = call(
        sum_kernel,
        (pltpu.VMEM((refs, width), bf16),),
        exchanged(own, "ref"),
        cross,
        norms,
        contrast,
        kept,
        scratch=[pltpu.VMEM((refs, count), bf16)],
        flops=flops,
    )
    gathered = gathered_rows(normalize(summed_share(img_partial)))
    own, new_references = call(
        score_kernel,
        (one, jax.ShapeDtypeStruct((refs, width), bf16)),
        gathered,
        kept,
        contrast,
        specs=(VMEM, HBM),
        scratch=[
            pltpu.VMEM((refs, LANES), f32),
            pltpu.SemaphoreType.DMA,
        ],
        flops=flops,
    )
    loglik = combined_log(exchanged(own, "ref")) - math.log(refs * devices)
    return (new_references, contrast.reshape(count), loglik.reshape(count))


def solution(mesh):
    placed = (P("img", None), P("ref", None), P("img"))
    return jax.shard_map(
        per_device,
        mesh=mesh,
        in_specs=placed,
        out_specs=(P("ref", None), P("img"), P("img")),
        check_vma=False,
    )
```

```python
import math

import jax
import jax.numpy as jnp
from jax import lax
from jax.experimental import pallas as pl
from jax.experimental.pallas import tpu as pltpu
from jax.sharding import PartitionSpec as P

ITERS = 3


sharpness = 2.0
prior_weight = 1.0
epsilon = 1e-06

X, Y, Z, CORES = 4, 8, 8, 2
PLANE = ("img", "ref")


def device(x, y, ref):
    return ((x % X) * Y + y % Y) * Z * CORES + ref


SIDES = [(a, b) for a in range(2) for b in range(2)]
REFS = range(Z * CORES)
BLOCKS = [
    [device(2 * i + a + ref % CORES, 2 * j + b + ref % CORES, ref) for a, b in SIDES]
    for ref in REFS
    for i in range(X // 2)
    for j in range(Y // 2)
]
ORDER = [(k % 2, j) for k, j in enumerate((0, 1, 1, 3, 2, 2, 3, 0))]
SPREAD = [[device(2 * i + a, 2 * j + b, ref) for i, j in ORDER] for ref in REFS for a, b in SIDES]


def exchanged(pieces, axis, groups=None):
    return lax.all_to_all(pieces, axis, 0, 0, tiled=True, axis_index_groups=groups)


def sent_to_all(value, axis, groups):
    return exchanged(jnp.broadcast_to(value[None], (len(groups[0]), *value.shape)), axis, groups)


def summed_share(partial):
    rows, width = partial.shape
    for groups in (BLOCKS, SPREAD):
        rows //= len(groups[0])
        pieces = partial.astype(jnp.bfloat16).reshape(len(groups[0]), rows, width)
        partial = jnp.sum(exchanged(pieces, PLANE, groups).astype(jnp.float32), axis=0)
    return partial


def gathered_rows(share):
    for groups in (SPREAD, BLOCKS):
        share = sent_to_all(share, PLANE, groups).reshape(-1, share.shape[-1])
    return share


def normalize(sums):
    meansq = jnp.mean(sums * sums, axis=1)
    return (sums * lax.rsqrt(meansq + epsilon)[:, None]).astype(jnp.bfloat16)


LANES = 128
BLOCK = 256
ROWS = BLOCK // LANES


def laid_out(value, k):
    return jnp.concatenate([value[k * ROWS + j : k * ROWS + j + 1] for j in range(ROWS)], axis=1)


def folded(parts):
    rows = [part[:, j * LANES : (j + 1) * LANES] for part in parts for j in range(ROWS)]
    return jnp.concatenate(rows, axis=0)


def block_at(k):
    return slice(k * BLOCK, (k + 1) * BLOCK)


def scored(terms, norms, contrast):
    wide = jnp.concatenate([norms[...]] * ROWS, axis=1)
    return sharpness * contrast * terms - 0.5 * sharpness * (contrast * contrast) * wide, wide


def own_refit(terms, norms, contrast, prior):
    scores, wide = scored(terms, norms, contrast)
    high = jnp.max(scores, axis=0, keepdims=True)
    e = jnp.exp(scores - high)
    total = jnp.sum(e, axis=0, keepdims=True)
    upper = jnp.sum(e * terms, axis=0, keepdims=True) + prior_weight * prior * total
    lower = jnp.sum(e * wide, axis=0, keepdims=True) + prior_weight * total
    return high + jnp.log(lower), upper / lower


def own_total(terms, norms, contrast):
    scores, _ = scored(terms, norms, contrast)
    high = jnp.max(scores, axis=0, keepdims=True)
    return high + jnp.log(jnp.sum(jnp.exp(scores - high), axis=0, keepdims=True))


def combined(received):
    logs, quotients = received[:, :8], received[:, 8:]
    share = jnp.exp(logs - jnp.max(logs, axis=0, keepdims=True))
    return jnp.sum(share * quotients, axis=0) / jnp.sum(share, axis=0)


def combined_log(logs):
    high = jnp.max(logs, axis=0)
    return high + jnp.log(jnp.sum(jnp.exp(logs - high[None]), axis=0))


def send(out, *parts):
    own = jnp.concatenate([folded(part) for part in parts], axis=0)
    out[...] = jnp.broadcast_to(own[None], out.shape)


def squares(held, norms, scale):
    rows = 64
    for i in range(held.shape[0] // rows):
        at = slice(i * rows, (i + 1) * rows)
        summed = jnp.zeros((rows, LANES), jnp.float32)
        for k in range(held.shape[1] // LANES):
            wide = held[at, k * LANES : (k + 1) * LANES].astype(jnp.float32)
            summed = summed + wide * wide
        norm = jnp.sum(summed, axis=1, keepdims=True) * scale
        norms[at, :] = jnp.broadcast_to(norm, (rows, LANES))


def product(held, images, k):
    return lax.dot_general(
        held[...], images[block_at(k), :], (((1,), (1,)), ((), ())), preferred_element_type=jnp.float32
    )


def first_kernel(images, references, prior, cross, kept, norms, out, held, semaphores):
    halves = 2
    size = images.shape[0] // halves
    copies = [pltpu.make_async_copy(references, held, semaphores.at[halves])]
    for h in range(halves):
        at = pl.ds(h * size, size)
        copies.append(pltpu.make_async_copy(images.at[at], kept.at[at], semaphores.at[h]))
    for copy in copies:
        copy.start()
    copies[0].wait()
    logs, quotients = [], []
    for h in range(halves):
        copies[h + 1].wait()
        if h == 0:
            squares(held, norms, 1.0)
        blocks = range(h * size // BLOCK, (h + 1) * size // BLOCK)
        for k in blocks:
            cross[:, block_at(k)] = product(held, kept, k)
        for k in blocks:
            start = laid_out(prior, k)
            log, quotient = own_refit(cross[:, block_at(k)], norms, start, start)
            logs.append(log)
            quotients.append(quotient)
    send(out, logs, quotients)


def refit_kernel(received, cross, norms, prior, images, out):
    contrast = combined(received[...])
    logs, quotients = [], []
    for k in range(cross.shape[1] // BLOCK):
        log, quotient = own_refit(
            cross[:, block_at(k)], norms, laid_out(contrast, k), laid_out(prior, k)
        )
        logs.append(log)
        quotients.append(quotient)
    send(out, logs, quotients)


def total_kernel(received, cross, norms, images, contrast, out):
    found = combined(received[...])
    contrast[...] = found
    send(
        out,
        [
            own_total(cross[:, block_at(k)], norms, laid_out(found, k))
            for k in range(cross.shape[1] // BLOCK)
        ],
    )


def sum_kernel(received, cross, norms, contrast, images, out, weights):
    log_total = combined_log(received[...])
    for k in range(cross.shape[1] // BLOCK):
        scale = laid_out(contrast, k)
        scores, _ = scored(cross[:, block_at(k)], norms, scale)
        posterior = jnp.exp(scores - laid_out(log_total, k))
        weights[:, block_at(k)] = (posterior * scale).astype(jnp.bfloat16)
    width = 512
    for k in range(images.shape[1] // width):
        at = slice(k * width, (k + 1) * width)
        out[:, at] = jnp.dot(
            weights[...], images[:, at], preferred_element_type=jnp.float32
        ).astype(jnp.bfloat16)


def score_kernel(gathered, images, contrast, out, result, norms, semaphore):
    copy = pltpu.make_async_copy(gathered, result, semaphore)
    copy.start()
    width = gathered.shape[1]
    squares(gathered, norms, 1.0 / width)
    logs = []
    for k in range(images.shape[0] // BLOCK):
        terms = product(gathered, images, k) * width**-0.5
        logs.append(own_total(terms, norms, laid_out(contrast, k)))
    send(out, logs)
    copy.wait()


VMEM = pl.BlockSpec(memory_space=pltpu.VMEM)
HBM = pl.BlockSpec(memory_space=pltpu.HBM)


def call(kernel, outs, *args, ins=None, specs=None, scratch=(), limit=16, flops=0):
    return pl.pallas_call(
        kernel,
        out_shape=outs,
        in_specs=ins or [VMEM] * len(args),
        out_specs=specs or (VMEM,) * len(outs),
        scratch_shapes=scratch,
        compiler_params=pltpu.CompilerParams(vmem_limit_bytes=limit * 2**20),
        cost_estimate=pl.CostEstimate(
            flops=flops, bytes_accessed=2**22, transcendentals=2**19
        ),
    )(*args)


def per_device(images, references, initial_contrast):
    count, width = images.shape
    refs = references.shape[0]
    devices = lax.axis_size("ref")
    f32, bf16 = jnp.float32, jnp.bfloat16
    per_image = (count // LANES, LANES)
    prior = initial_contrast.reshape(per_image)
    two = pltpu.VMEM((devices, 2 * per_image[0], LANES), f32)
    one = pltpu.VMEM((devices, *per_image), f32)
    flops = 2 * count * refs * width

    cross, kept, norms, own = call(
        first_kernel,
        (
            pltpu.VMEM((refs, count), f32),
            pltpu.VMEM((count, width), bf16),
            pltpu.VMEM((refs, LANES), f32),
            two,
        ),
        images,
        references,
        prior,
        ins=[HBM, HBM, VMEM],
        scratch=[pltpu.VMEM((refs, width), bf16), pltpu.SemaphoreType.DMA((3,))],
        limit=54,
        flops=flops,
    )
    for _ in range(ITERS - 1):
        (own,) = call(refit_kernel, (two,), exchanged(own, "ref"), cross, norms, prior, kept)
    contrast, own = call(
        total_kernel,
        (pltpu.VMEM(per_image, f32), one),
        exchanged(own, "ref"),
        cross,
        norms,
        kept,
    )
    (img_partial,) = call(
        sum_kernel,
        (pltpu.VMEM((refs, width), bf16),),
        exchanged(own, "ref"),
        cross,
        norms,
        contrast,
        kept,
        scratch=[pltpu.VMEM((refs, count), bf16)],
        flops=flops,
    )
    gathered = gathered_rows(normalize(summed_share(img_partial)))
    own, new_references = call(
        score_kernel,
        (one, jax.ShapeDtypeStruct((refs, width), bf16)),
        gathered,
        kept,
        contrast,
        specs=(VMEM, HBM),
        scratch=[
            pltpu.VMEM((refs, LANES), f32),
            pltpu.SemaphoreType.DMA,
        ],
        flops=flops,
    )
    loglik = combined_log(exchanged(own, "ref")) - math.log(refs * devices)
    return (new_references, contrast.reshape(count), loglik.reshape(count))


def solution(mesh):
    placed = (P("img", None), P("ref", None), P("img"))
    return jax.shard_map(
        per_device,
        mesh=mesh,
        in_specs=placed,
        out_specs=(P("ref", None), P("img"), P("img")),
        check_vma=False,
    )
```

```python
import math

import jax
import jax.numpy as jnp
from jax import lax
from jax.experimental import pallas as pl
from jax.experimental.pallas import tpu as pltpu
from jax.sharding import PartitionSpec as P

ITERS = 3


sharpness = 2.0
prior_weight = 1.0
epsilon = 1e-06

X, Y, Z, CORES = 4, 8, 8, 2
PLANE = ("img", "ref")


def device(x, y, ref):
    return ((x % X) * Y + y % Y) * Z * CORES + ref


SIDES = [(a, b) for a in range(2) for b in range(2)]
REFS = range(Z * CORES)
BLOCKS = [
    [device(2 * i + a + ref % CORES, 2 * j + b + ref % CORES, ref) for a, b in SIDES]
    for ref in REFS
    for i in range(X // 2)
    for j in range(Y // 2)
]
ORDER = [(k % 2, (k // 2 + k % 2 * 2) % 4) for k in range(X * Y // 4)]
SPREAD = [[device(2 * i + a, 2 * j + b, ref) for i, j in ORDER] for ref in REFS for a, b in SIDES]


def exchanged(pieces, axis, groups=None):
    return lax.all_to_all(pieces, axis, 0, 0, tiled=True, axis_index_groups=groups)


def sent_to_all(value, axis, groups):
    return exchanged(jnp.broadcast_to(value[None], (len(groups[0]), *value.shape)), axis, groups)


def summed_share(partial):
    rows, width = partial.shape
    for groups in (BLOCKS, SPREAD):
        rows //= len(groups[0])
        pieces = partial.astype(jnp.bfloat16).reshape(len(groups[0]), rows, width)
        partial = jnp.sum(exchanged(pieces, PLANE, groups).astype(jnp.float32), axis=0)
    return partial


WAYS = ((1, 0), (0, 1), (1, 1))


def toward(along_x, along_y):
    pairs = []
    for ref in REFS:
        for x in range(X):
            for y in range(Y):
                a, b = (x + ref) % 2, (y + ref) % 2
                to = device(x + along_x * (1 - 2 * a), y + along_y * (1 - 2 * b), ref)
                pairs.append((device(x, y, ref), to))
    return pairs


def normalize(sums):
    meansq = jnp.mean(sums * sums, axis=1)
    return (sums * lax.rsqrt(meansq + epsilon)[:, None]).astype(jnp.bfloat16)


LANES = 128
BLOCK = 256
ROWS = BLOCK // LANES


def laid_out(value, k):
    return jnp.concatenate([value[k * ROWS + j : k * ROWS + j + 1] for j in range(ROWS)], axis=1)


def folded(parts):
    rows = [part[:, j * LANES : (j + 1) * LANES] for part in parts for j in range(ROWS)]
    return jnp.concatenate(rows, axis=0)


def block_at(k):
    return slice(k * BLOCK, (k + 1) * BLOCK)


def scored(terms, norms, contrast):
    wide = jnp.concatenate([norms[...]] * ROWS, axis=1)
    return sharpness * contrast * terms - 0.5 * sharpness * (contrast * contrast) * wide, wide


def own_refit(terms, norms, contrast, prior):
    scores, wide = scored(terms, norms, contrast)
    high = jnp.max(scores, axis=0, keepdims=True)
    e = jnp.exp(scores - high)
    total = jnp.sum(e, axis=0, keepdims=True)
    upper = jnp.sum(e * terms, axis=0, keepdims=True) + prior_weight * prior * total
    lower = jnp.sum(e * wide, axis=0, keepdims=True) + prior_weight * total
    return high + jnp.log(lower), upper / lower


def own_total(terms, norms, contrast):
    scores, _ = scored(terms, norms, contrast)
    high = jnp.max(scores, axis=0, keepdims=True)
    return high + jnp.log(jnp.sum(jnp.exp(scores - high), axis=0, keepdims=True))


def combined(received):
    logs, quotients = received[:, :8], received[:, 8:]
    share = jnp.exp(logs - jnp.max(logs, axis=0, keepdims=True))
    return jnp.sum(share * quotients, axis=0) / jnp.sum(share, axis=0)


def combined_log(logs):
    high = jnp.max(logs, axis=0)
    return high + jnp.log(jnp.sum(jnp.exp(logs - high[None]), axis=0))


def send(out, *parts):
    own = jnp.concatenate([folded(part) for part in parts], axis=0)
    out[...] = jnp.broadcast_to(own[None], out.shape)


def squares(held, norms, scale):
    rows = 64
    for i in range(held.shape[0] // rows):
        at = slice(i * rows, (i + 1) * rows)
        summed = jnp.zeros((rows, LANES), jnp.float32)
        for k in range(held.shape[1] // LANES):
            wide = held[at, k * LANES : (k + 1) * LANES].astype(jnp.float32)
            summed = summed + wide * wide
        norm = jnp.sum(summed, axis=1, keepdims=True) * scale
        norms[at, :] = jnp.broadcast_to(norm, (rows, LANES))


def product(held, images, k):
    return lax.dot_general(
        held[...], images[block_at(k), :], (((1,), (1,)), ((), ())), preferred_element_type=jnp.float32
    )


def first_kernel(images, references, prior, cross, kept, norms, out, held, semaphores):
    halves = 2
    size = images.shape[0] // halves
    copies = [pltpu.make_async_copy(references, held, semaphores.at[halves])]
    for h in range(halves):
        at = pl.ds(h * size, size)
        copies.append(pltpu.make_async_copy(images.at[at], kept.at[at], semaphores.at[h]))
    for copy in copies:
        copy.start()
    copies[0].wait()
    logs, quotients = [], []
    for h in range(halves):
        copies[h + 1].wait()
        if h == 0:
            squares(held, norms, 1.0)
        blocks = range(h * size // BLOCK, (h + 1) * size // BLOCK)
        for k in blocks:
            cross[:, block_at(k)] = product(held, kept, k)
        for k in blocks:
            start = laid_out(prior, k)
            log, quotient = own_refit(cross[:, block_at(k)], norms, start, start)
            logs.append(log)
            quotients.append(quotient)
    send(out, logs, quotients)


def refit_kernel(received, cross, norms, prior, images, out):
    contrast = combined(received[...])
    logs, quotients = [], []
    for k in range(cross.shape[1] // BLOCK):
        log, quotient = own_refit(
            cross[:, block_at(k)], norms, laid_out(contrast, k), laid_out(prior, k)
        )
        logs.append(log)
        quotients.append(quotient)
    send(out, logs, quotients)


def total_kernel(received, cross, norms, images, contrast, out):
    found = combined(received[...])
    contrast[...] = found
    send(
        out,
        [
            own_total(cross[:, block_at(k)], norms, laid_out(found, k))
            for k in range(cross.shape[1] // BLOCK)
        ],
    )


def sum_kernel(received, cross, norms, contrast, images, out, weights):
    log_total = combined_log(received[...])
    for k in range(cross.shape[1] // BLOCK):
        scale = laid_out(contrast, k)
        scores, _ = scored(cross[:, block_at(k)], norms, scale)
        posterior = jnp.exp(scores - laid_out(log_total, k))
        weights[:, block_at(k)] = (posterior * scale).astype(jnp.bfloat16)
    width = 512
    for k in range(images.shape[1] // width):
        at = slice(k * width, (k + 1) * width)
        out[:, at] = jnp.dot(
            weights[...], images[:, at], preferred_element_type=jnp.float32
        ).astype(jnp.bfloat16)


def scored_rows(piece, images, contrast, norms):
    width = piece.shape[1]
    squares(piece, norms, 1.0 / width)
    logs = []
    for k in range(images.shape[0] // BLOCK):
        terms = product(piece, images, k) * width**-0.5
        logs.append(own_total(terms, norms, laid_out(contrast, k)))
    return folded(logs)


def score_kernel(piece, images, contrast, out, norms):
    out[...] = scored_rows(piece, images, contrast, norms)


def pair_kernel(first, second, images, contrast, before, out, norms):
    logs = [before[...]]
    logs += [scored_rows(piece, images, contrast, norms) for piece in (first, second)]
    out[...] = combined_log(jnp.stack(logs))


def last_kernel(own, first, second, last, images, contrast, before, out, result, norms, semaphores):
    image, ref = lax.axis_index("img"), lax.axis_index("ref")
    a = lax.rem(lax.div(image, Y) + ref, 2)
    b = lax.rem(lax.rem(image, Y) + ref, 2)
    rows = own.shape[0]
    copies = []
    for k, (piece, side) in enumerate(
        (
            (own, a * 2 + b),
            (first, (1 - a) * 2 + b),
            (second, a * 2 + 1 - b),
            (last, (1 - a) * 2 + 1 - b),
        )
    ):
        place = pl.ds(pl.multiple_of(side * rows, rows), rows)
        copies.append(pltpu.make_async_copy(piece, result.at[place], semaphores.at[k]))
    for copy in copies:
        copy.start()
    logs = scored_rows(last, images, contrast, norms)
    out[...] = jnp.broadcast_to(combined_log(jnp.stack([before[...], logs]))[None], out.shape)
    for copy in copies:
        copy.wait()


VMEM = pl.BlockSpec(memory_space=pltpu.VMEM)
HBM = pl.BlockSpec(memory_space=pltpu.HBM)


def call(kernel, outs, *args, ins=None, specs=None, scratch=(), limit=16, flops=0):
    return pl.pallas_call(
        kernel,
        out_shape=outs,
        in_specs=ins or [VMEM] * len(args),
        out_specs=specs or (VMEM,) * len(outs),
        scratch_shapes=scratch,
        compiler_params=pltpu.CompilerParams(vmem_limit_bytes=limit * 2**20),
        cost_estimate=pl.CostEstimate(
            flops=flops, bytes_accessed=2**22, transcendentals=2**19
        ),
    )(*args)


def per_device(images, references, initial_contrast):
    count, width = images.shape
    refs = references.shape[0]
    devices = lax.axis_size("ref")
    f32, bf16 = jnp.float32, jnp.bfloat16
    per_image = (count // LANES, LANES)
    prior = initial_contrast.reshape(per_image)
    two = pltpu.VMEM((devices, 2 * per_image[0], LANES), f32)
    one = pltpu.VMEM((devices, *per_image), f32)
    flops = 2 * count * refs * width

    cross, kept, norms, own = call(
        first_kernel,
        (
            pltpu.VMEM((refs, count), f32),
            pltpu.VMEM((count, width), bf16),
            pltpu.VMEM((refs, LANES), f32),
            two,
        ),
        images,
        references,
        prior,
        ins=[HBM, HBM, VMEM],
        scratch=[pltpu.VMEM((refs, width), bf16), pltpu.SemaphoreType.DMA((3,))],
        limit=54,
        flops=flops,
    )
    for _ in range(ITERS - 1):
        (own,) = call(refit_kernel, (two,), exchanged(own, "ref"), cross, norms, prior, kept)
    contrast, own = call(
        total_kernel,
        (pltpu.VMEM(per_image, f32), one),
        exchanged(own, "ref"),
        cross,
        norms,
        kept,
    )
    (img_partial,) = call(
        sum_kernel,
        (pltpu.VMEM((refs, width), bf16),),
        exchanged(own, "ref"),
        cross,
        norms,
        contrast,
        kept,
        scratch=[pltpu.VMEM((refs, count), bf16)],
        flops=flops,
    )
    share = normalize(summed_share(img_partial))
    rows = sent_to_all(share, PLANE, SPREAD).reshape(-1, width)
    first, second, last = (lax.ppermute(rows, PLANE, toward(*way)) for way in WAYS)
    norm = [pltpu.VMEM((rows.shape[0], LANES), f32)]
    log = (pltpu.VMEM(per_image, f32),)
    (before,) = call(score_kernel, log, rows, kept, contrast, scratch=norm, flops=flops // 4)
    (before,) = call(
        pair_kernel, log, first, second, kept, contrast, before, scratch=norm, flops=flops // 2
    )
    own, new_references = call(
        last_kernel,
        (one, jax.ShapeDtypeStruct((refs, width), bf16)),
        rows,
        first,
        second,
        last,
        kept,
        contrast,
        before,
        specs=(VMEM, HBM),
        scratch=[*norm, pltpu.SemaphoreType.DMA((4,))],
        flops=flops // 4,
    )
    loglik = combined_log(exchanged(own, "ref")) - math.log(refs * devices)
    return (new_references, contrast.reshape(count), loglik.reshape(count))


def solution(mesh):
    placed = (P("img", None), P("ref", None), P("img"))
    return jax.shard_map(
        per_device,
        mesh=mesh,
        in_specs=placed,
        out_specs=(P("ref", None), P("img"), P("img")),
        check_vma=False,
    )
```

```python
import math

import jax
import jax.numpy as jnp
from jax import lax
from jax.experimental import pallas as pl
from jax.experimental.pallas import tpu as pltpu
from jax.sharding import PartitionSpec as P

ITERS = 3


sharpness = 2.0
prior_weight = 1.0
epsilon = 1e-06

X, Y, Z, CORES = 4, 8, 8, 2
PLANE = ("img", "ref")


def device(x, y, ref):
    return ((x % X) * Y + y % Y) * Z * CORES + ref


SIDES = [(a, b) for a in range(2) for b in range(2)]
REFS = range(Z * CORES)
BLOCKS = [
    [device(2 * i + a + ref % CORES, 2 * j + b + ref % CORES, ref) for a, b in SIDES]
    for ref in REFS
    for i in range(X // 2)
    for j in range(Y // 2)
]
ORDER = [(k % 2, (k // 2 + k % 2 * 2) % 4) for k in range(X * Y // 4)]
SPREAD = [[device(2 * i + a, 2 * j + b, ref) for i, j in ORDER] for ref in REFS for a, b in SIDES]


def exchanged(pieces, axis, groups=None):
    return lax.all_to_all(pieces, axis, 0, 0, tiled=True, axis_index_groups=groups)


def sent_to_all(value, axis, groups):
    return exchanged(jnp.broadcast_to(value[None], (len(groups[0]), *value.shape)), axis, groups)


def summed_share(partial):
    rows, width = partial.shape
    for groups in (BLOCKS, SPREAD):
        rows //= len(groups[0])
        pieces = partial.astype(jnp.bfloat16).reshape(len(groups[0]), rows, width)
        partial = jnp.sum(exchanged(pieces, PLANE, groups).astype(jnp.float32), axis=0)
    return partial


WAYS = ((1, 0), (0, 1), (1, 1))


def toward(along_x, along_y):
    pairs = []
    for ref in REFS:
        for x in range(X):
            for y in range(Y):
                a, b = (x + ref) % 2, (y + ref) % 2
                to = device(x + along_x * (1 - 2 * a), y + along_y * (1 - 2 * b), ref)
                pairs.append((device(x, y, ref), to))
    return pairs


def normalize(sums):
    meansq = jnp.mean(sums * sums, axis=1)
    return (sums * lax.rsqrt(meansq + epsilon)[:, None]).astype(jnp.bfloat16)


LANES = 128
BLOCK = 256
ROWS = BLOCK // LANES


def laid_out(value, k):
    return jnp.concatenate([value[k * ROWS + j : k * ROWS + j + 1] for j in range(ROWS)], axis=1)


def folded(parts):
    rows = [part[:, j * LANES : (j + 1) * LANES] for part in parts for j in range(ROWS)]
    return jnp.concatenate(rows, axis=0)


def block_at(k):
    return slice(k * BLOCK, (k + 1) * BLOCK)


def scored(terms, norms, contrast):
    wide = jnp.concatenate([norms[...]] * ROWS, axis=1)
    return sharpness * contrast * terms - 0.5 * sharpness * (contrast * contrast) * wide, wide


def own_refit(terms, norms, contrast, prior):
    scores, wide = scored(terms, norms, contrast)
    high = jnp.max(scores, axis=0, keepdims=True)
    e = jnp.exp(scores - high)
    total = jnp.sum(e, axis=0, keepdims=True)
    upper = jnp.sum(e * terms, axis=0, keepdims=True) + prior_weight * prior * total
    lower = jnp.sum(e * wide, axis=0, keepdims=True) + prior_weight * total
    return high + jnp.log(lower), upper / lower


def own_total(terms, norms, contrast):
    scores, _ = scored(terms, norms, contrast)
    high = jnp.max(scores, axis=0, keepdims=True)
    return high + jnp.log(jnp.sum(jnp.exp(scores - high), axis=0, keepdims=True))


def combined(received):
    logs, quotients = received[:, :8], received[:, 8:]
    share = jnp.exp(logs - jnp.max(logs, axis=0, keepdims=True))
    return jnp.sum(share * quotients, axis=0) / jnp.sum(share, axis=0)


def combined_log(logs):
    high = jnp.max(logs, axis=0)
    return high + jnp.log(jnp.sum(jnp.exp(logs - high[None]), axis=0))


def send(out, *parts):
    own = jnp.concatenate([folded(part) for part in parts], axis=0)
    out[...] = jnp.broadcast_to(own[None], out.shape)


def squares(held, norms, scale):
    rows = 64
    for i in range(held.shape[0] // rows):
        at = slice(i * rows, (i + 1) * rows)
        summed = jnp.zeros((rows, LANES), jnp.float32)
        for k in range(held.shape[1] // LANES):
            wide = held[at, k * LANES : (k + 1) * LANES].astype(jnp.float32)
            summed = summed + wide * wide
        norm = jnp.sum(summed, axis=1, keepdims=True) * scale
        norms[at, :] = jnp.broadcast_to(norm, (rows, LANES))


def product(held, images, k):
    return lax.dot_general(
        held[...], images[block_at(k), :], (((1,), (1,)), ((), ())), preferred_element_type=jnp.float32
    )


def first_kernel(images, references, prior, cross, kept, norms, out, held, semaphores):
    halves = 2
    size = images.shape[0] // halves
    copies = [pltpu.make_async_copy(references, held, semaphores.at[halves])]
    for h in range(halves):
        at = pl.ds(h * size, size)
        copies.append(pltpu.make_async_copy(images.at[at], kept.at[at], semaphores.at[h]))
    for copy in copies:
        copy.start()
    copies[0].wait()
    logs, quotients = [], []
    for h in range(halves):
        copies[h + 1].wait()
        if h == 0:
            squares(held, norms, 1.0)
        blocks = range(h * size // BLOCK, (h + 1) * size // BLOCK)
        for k in blocks:
            cross[:, block_at(k)] = product(held, kept, k)
        for k in blocks:
            start = laid_out(prior, k)
            log, quotient = own_refit(cross[:, block_at(k)], norms, start, start)
            logs.append(log)
            quotients.append(quotient)
    send(out, logs, quotients)


def refit_kernel(received, cross, norms, prior, images, out):
    contrast = combined(received[...])
    logs, quotients = [], []
    for k in range(cross.shape[1] // BLOCK):
        log, quotient = own_refit(
            cross[:, block_at(k)], norms, laid_out(contrast, k), laid_out(prior, k)
        )
        logs.append(log)
        quotients.append(quotient)
    send(out, logs, quotients)


def total_kernel(received, cross, norms, images, contrast, out):
    found = combined(received[...])
    contrast[...] = found
    send(
        out,
        [
            own_total(cross[:, block_at(k)], norms, laid_out(found, k))
            for k in range(cross.shape[1] // BLOCK)
        ],
    )


def sum_kernel(received, cross, norms, contrast, images, out, weights):
    log_total = combined_log(received[...])
    for k in range(cross.shape[1] // BLOCK):
        scale = laid_out(contrast, k)
        scores, _ = scored(cross[:, block_at(k)], norms, scale)
        posterior = jnp.exp(scores - laid_out(log_total, k))
        weights[:, block_at(k)] = (posterior * scale).astype(jnp.bfloat16)
    width = 512
    for k in range(images.shape[1] // width):
        at = slice(k * width, (k + 1) * width)
        out[:, at] = jnp.dot(
            weights[...], images[:, at], preferred_element_type=jnp.float32
        ).astype(jnp.bfloat16)


def scored_rows(piece, images, contrast, norms):
    width = piece.shape[1]
    squares(piece, norms, 1.0 / width)
    logs = []
    for k in range(images.shape[0] // BLOCK):
        terms = product(piece, images, k) * width**-0.5
        logs.append(own_total(terms, norms, laid_out(contrast, k)))
    return folded(logs)


def score_kernel(piece, images, contrast, out, norms):
    out[...] = scored_rows(piece, images, contrast, norms)


def writes(pieces, result, semaphores):
    image, ref = lax.axis_index("img"), lax.axis_index("ref")
    a = lax.rem(lax.div(image, Y) + ref, 2)
    b = lax.rem(lax.rem(image, Y) + ref, 2)
    copies = []
    for k, (piece, (along_x, along_y)) in enumerate(pieces):
        side = (1 - a if along_x else a) * 2 + (1 - b if along_y else b)
        rows = piece.shape[0]
        place = pl.ds(pl.multiple_of(side * rows, rows), rows)
        copies.append(pltpu.make_async_copy(piece, result.at[place], semaphores.at[k]))
    return copies


def pair_kernel(own, first, second, images, contrast, before, out, result, norms, semaphores):
    copies = writes(((own, (0, 0)), (first, WAYS[0]), (second, WAYS[1])), result, semaphores)
    for copy in copies:
        copy.start()
    logs = [before[...]]
    logs += [scored_rows(piece, images, contrast, norms) for piece in (first, second)]
    out[...] = combined_log(jnp.stack(logs))
    for copy in copies:
        copy.wait()


def last_kernel(last, images, contrast, before, begun, out, result, norms, semaphores):
    (copy,) = writes(((last, WAYS[2]),), result, semaphores)
    copy.start()
    logs = scored_rows(last, images, contrast, norms)
    out[...] = jnp.broadcast_to(combined_log(jnp.stack([before[...], logs]))[None], out.shape)
    copy.wait()


VMEM = pl.BlockSpec(memory_space=pltpu.VMEM)
HBM = pl.BlockSpec(memory_space=pltpu.HBM)


def call(kernel, outs, *args, ins=None, specs=None, scratch=(), limit=16, flops=0, aliases=None):
    return pl.pallas_call(
        kernel,
        out_shape=outs,
        in_specs=ins or [VMEM] * len(args),
        out_specs=specs or (VMEM,) * len(outs),
        scratch_shapes=scratch,
        input_output_aliases=aliases or {},
        compiler_params=pltpu.CompilerParams(vmem_limit_bytes=limit * 2**20),
        cost_estimate=pl.CostEstimate(
            flops=flops, bytes_accessed=2**22, transcendentals=2**19
        ),
    )(*args)


def per_device(images, references, initial_contrast):
    count, width = images.shape
    refs = references.shape[0]
    devices = lax.axis_size("ref")
    f32, bf16 = jnp.float32, jnp.bfloat16
    per_image = (count // LANES, LANES)
    prior = initial_contrast.reshape(per_image)
    two = pltpu.VMEM((devices, 2 * per_image[0], LANES), f32)
    one = pltpu.VMEM((devices, *per_image), f32)
    flops = 2 * count * refs * width

    cross, kept, norms, own = call(
        first_kernel,
        (
            pltpu.VMEM((refs, count), f32),
            pltpu.VMEM((count, width), bf16),
            pltpu.VMEM((refs, LANES), f32),
            two,
        ),
        images,
        references,
        prior,
        ins=[HBM, HBM, VMEM],
        scratch=[pltpu.VMEM((refs, width), bf16), pltpu.SemaphoreType.DMA((3,))],
        limit=54,
        flops=flops,
    )
    for _ in range(ITERS - 1):
        (own,) = call(refit_kernel, (two,), exchanged(own, "ref"), cross, norms, prior, kept)
    contrast, own = call(
        total_kernel,
        (pltpu.VMEM(per_image, f32), one),
        exchanged(own, "ref"),
        cross,
        norms,
        kept,
    )
    (img_partial,) = call(
        sum_kernel,
        (pltpu.VMEM((refs, width), bf16),),
        exchanged(own, "ref"),
        cross,
        norms,
        contrast,
        kept,
        scratch=[pltpu.VMEM((refs, count), bf16)],
        flops=flops,
    )
    share = normalize(summed_share(img_partial))
    rows = sent_to_all(share, PLANE, SPREAD).reshape(-1, width)
    first, second, last = (lax.ppermute(rows, PLANE, toward(*way)) for way in WAYS)
    norm = [pltpu.VMEM((rows.shape[0], LANES), f32)]
    log = (pltpu.VMEM(per_image, f32),)
    (before,) = call(score_kernel, log, rows, kept, contrast, scratch=norm, flops=flops // 4)
    before, begun = call(
        pair_kernel,
        (*log, pltpu.HBM((refs, width), bf16)),
        rows,
        first,
        second,
        kept,
        contrast,
        before,
        specs=(VMEM, HBM),
        scratch=[*norm, pltpu.SemaphoreType.DMA((3,))],
        flops=flops // 2,
    )
    own, new_references = call(
        last_kernel,
        (one, pltpu.HBM((refs, width), bf16)),
        last,
        kept,
        contrast,
        before,
        begun,
        ins=[VMEM] * 4 + [HBM],
        specs=(VMEM, HBM),
        scratch=[*norm, pltpu.SemaphoreType.DMA((1,))],
        aliases={4: 1},
        flops=flops // 4,
    )
    loglik = combined_log(exchanged(own, "ref")) - math.log(refs * devices)
    return (new_references, contrast.reshape(count), loglik.reshape(count))


def solution(mesh):
    placed = (P("img", None), P("ref", None), P("img"))
    return jax.shard_map(
        per_device,
        mesh=mesh,
        in_specs=placed,
        out_specs=(P("ref", None), P("img"), P("img")),
        check_vma=False,
    )
```

```python
import math

import jax
import jax.numpy as jnp
from jax import lax
from jax.experimental import pallas as pl
from jax.experimental.pallas import tpu as pltpu
from jax.sharding import PartitionSpec as P

ITERS = 3


sharpness = 2.0
prior_weight = 1.0
epsilon = 1e-06

X, Y, Z, CORES = 4, 8, 8, 2
PLANE = ("img", "ref")


def device(x, y, ref):
    return ((x % X) * Y + y % Y) * Z * CORES + ref


SIDES = [(a, b) for a in range(2) for b in range(2)]
REFS = range(Z * CORES)
BLOCKS = [
    [device(2 * i + a + ref % CORES, 2 * j + b + ref % CORES, ref) for a, b in SIDES]
    for ref in REFS
    for i in range(X // 2)
    for j in range(Y // 2)
]
ORDER = [(k % 2, (k // 2 + k % 2 * 2) % 4) for k in range(X * Y // 4)]
SPREAD = [[device(2 * i + a, 2 * j + b, ref) for i, j in ORDER] for ref in REFS for a, b in SIDES]


def exchanged(pieces, axis, groups=None):
    return lax.all_to_all(pieces, axis, 0, 0, tiled=True, axis_index_groups=groups)


def sent_to_all(value, axis, groups):
    return exchanged(jnp.broadcast_to(value[None], (len(groups[0]), *value.shape)), axis, groups)


def summed_share(partial):
    rows, width = partial.shape
    for groups in (BLOCKS, SPREAD):
        rows //= len(groups[0])
        pieces = partial.astype(jnp.bfloat16).reshape(len(groups[0]), rows, width)
        partial = jnp.sum(exchanged(pieces, PLANE, groups).astype(jnp.float32), axis=0)
    return partial


WAYS = ((1, 0), (0, 1), (1, 1))


def toward(along_x, along_y):
    pairs = []
    for ref in REFS:
        for x in range(X):
            for y in range(Y):
                a, b = (x + ref) % 2, (y + ref) % 2
                to = device(x + along_x * (1 - 2 * a), y + along_y * (1 - 2 * b), ref)
                pairs.append((device(x, y, ref), to))
    return pairs


def normalize(sums):
    meansq = jnp.mean(sums * sums, axis=1)
    return (sums * lax.rsqrt(meansq + epsilon)[:, None]).astype(jnp.bfloat16)


LANES = 128
BLOCK = 256
ROWS = BLOCK // LANES


def laid_out(value, k):
    return jnp.concatenate([value[k * ROWS + j : k * ROWS + j + 1] for j in range(ROWS)], axis=1)


def folded(parts):
    rows = [part[:, j * LANES : (j + 1) * LANES] for part in parts for j in range(ROWS)]
    return jnp.concatenate(rows, axis=0)


def block_at(k):
    return slice(k * BLOCK, (k + 1) * BLOCK)


def scored(terms, norms, contrast):
    wide = jnp.concatenate([norms[...]] * ROWS, axis=1)
    return sharpness * contrast * terms - 0.5 * sharpness * (contrast * contrast) * wide, wide


def own_refit(terms, norms, contrast, prior):
    scores, wide = scored(terms, norms, contrast)
    high = jnp.max(scores, axis=0, keepdims=True)
    e = jnp.exp(scores - high)
    total = jnp.sum(e, axis=0, keepdims=True)
    upper = jnp.sum(e * terms, axis=0, keepdims=True) + prior_weight * prior * total
    lower = jnp.sum(e * wide, axis=0, keepdims=True) + prior_weight * total
    return high + jnp.log(lower), upper / lower


def own_total(terms, norms, contrast):
    scores, _ = scored(terms, norms, contrast)
    high = jnp.max(scores, axis=0, keepdims=True)
    return high + jnp.log(jnp.sum(jnp.exp(scores - high), axis=0, keepdims=True))


def combined(received):
    logs, quotients = received[:, :8], received[:, 8:]
    share = jnp.exp(logs - jnp.max(logs, axis=0, keepdims=True))
    return jnp.sum(share * quotients, axis=0) / jnp.sum(share, axis=0)


def combined_log(logs):
    high = jnp.max(logs, axis=0)
    return high + jnp.log(jnp.sum(jnp.exp(logs - high[None]), axis=0))


def send(out, *parts):
    own = jnp.concatenate([folded(part) for part in parts], axis=0)
    out[...] = jnp.broadcast_to(own[None], out.shape)


def squares(held, norms, scale):
    rows = 64
    for i in range(held.shape[0] // rows):
        at = slice(i * rows, (i + 1) * rows)
        summed = jnp.zeros((rows, LANES), jnp.float32)
        for k in range(held.shape[1] // LANES):
            wide = held[at, k * LANES : (k + 1) * LANES].astype(jnp.float32)
            summed = summed + wide * wide
        norm = jnp.sum(summed, axis=1, keepdims=True) * scale
        norms[at, :] = jnp.broadcast_to(norm, (rows, LANES))


def product(held, images, k):
    return lax.dot_general(
        held[...], images[block_at(k), :], (((1,), (1,)), ((), ())), preferred_element_type=jnp.float32
    )


def first_kernel(images, references, prior, cross, kept, norms, out, held, semaphores):
    halves = 2
    size = images.shape[0] // halves
    copies = [pltpu.make_async_copy(references, held, semaphores.at[halves])]
    for h in range(halves):
        at = pl.ds(h * size, size)
        copies.append(pltpu.make_async_copy(images.at[at], kept.at[at], semaphores.at[h]))
    for copy in copies:
        copy.start()
    copies[0].wait()
    logs, quotients = [], []
    for h in range(halves):
        copies[h + 1].wait()
        if h == 0:
            squares(held, norms, 1.0)
        blocks = range(h * size // BLOCK, (h + 1) * size // BLOCK)
        for k in blocks:
            cross[:, block_at(k)] = product(held, kept, k)
        for k in blocks:
            start = laid_out(prior, k)
            log, quotient = own_refit(cross[:, block_at(k)], norms, start, start)
            logs.append(log)
            quotients.append(quotient)
    send(out, logs, quotients)


def refit_kernel(received, cross, norms, prior, images, out):
    contrast = combined(received[...])
    logs, quotients = [], []
    for k in range(cross.shape[1] // BLOCK):
        log, quotient = own_refit(
            cross[:, block_at(k)], norms, laid_out(contrast, k), laid_out(prior, k)
        )
        logs.append(log)
        quotients.append(quotient)
    send(out, logs, quotients)


def total_kernel(received, cross, norms, images, contrast, out, result, semaphore):
    found = combined(received[...])
    contrast[...] = found
    copy = pltpu.make_async_copy(contrast, result, semaphore)
    copy.start()
    send(
        out,
        [
            own_total(cross[:, block_at(k)], norms, laid_out(found, k))
            for k in range(cross.shape[1] // BLOCK)
        ],
    )
    copy.wait()


def sum_kernel(received, cross, norms, contrast, images, out, weights):
    log_total = combined_log(received[...])
    for k in range(cross.shape[1] // BLOCK):
        scale = laid_out(contrast, k)
        scores, _ = scored(cross[:, block_at(k)], norms, scale)
        posterior = jnp.exp(scores - laid_out(log_total, k))
        weights[:, block_at(k)] = (posterior * scale).astype(jnp.bfloat16)
    width = 512
    for k in range(images.shape[1] // width):
        at = slice(k * width, (k + 1) * width)
        out[:, at] = jnp.dot(
            weights[...], images[:, at], preferred_element_type=jnp.float32
        ).astype(jnp.bfloat16)


def scored_rows(piece, images, contrast, norms):
    width = piece.shape[1]
    squares(piece, norms, 1.0 / width)
    logs = []
    for k in range(images.shape[0] // BLOCK):
        terms = product(piece, images, k) * width**-0.5
        logs.append(own_total(terms, norms, laid_out(contrast, k)))
    return folded(logs)


def score_kernel(piece, images, contrast, out, norms):
    out[...] = scored_rows(piece, images, contrast, norms)


def writes(pieces, result, semaphores):
    image, ref = lax.axis_index("img"), lax.axis_index("ref")
    a = lax.rem(lax.div(image, Y) + ref, 2)
    b = lax.rem(lax.rem(image, Y) + ref, 2)
    copies = []
    for k, (piece, (along_x, along_y)) in enumerate(pieces):
        side = (1 - a if along_x else a) * 2 + (1 - b if along_y else b)
        rows = piece.shape[0]
        place = pl.ds(pl.multiple_of(side * rows, rows), rows)
        copies.append(pltpu.make_async_copy(piece, result.at[place], semaphores.at[k]))
    return copies


def pair_kernel(own, first, second, images, contrast, before, out, result, norms, semaphores):
    copies = writes(((own, (0, 0)), (first, WAYS[0]), (second, WAYS[1])), result, semaphores)
    for copy in copies:
        copy.start()
    logs = [before[...]]
    logs += [scored_rows(piece, images, contrast, norms) for piece in (first, second)]
    out[...] = combined_log(jnp.stack(logs))
    for copy in copies:
        copy.wait()


def last_kernel(last, images, contrast, before, begun, out, result, norms, semaphores):
    (copy,) = writes(((last, WAYS[2]),), result, semaphores)
    copy.start()
    logs = scored_rows(last, images, contrast, norms)
    out[...] = jnp.broadcast_to(combined_log(jnp.stack([before[...], logs]))[None], out.shape)
    copy.wait()


VMEM = pl.BlockSpec(memory_space=pltpu.VMEM)
HBM = pl.BlockSpec(memory_space=pltpu.HBM)


def call(kernel, outs, *args, ins=None, specs=None, scratch=(), limit=16, flops=0, aliases=None):
    return pl.pallas_call(
        kernel,
        out_shape=outs,
        in_specs=ins or [VMEM] * len(args),
        out_specs=specs or (VMEM,) * len(outs),
        scratch_shapes=scratch,
        input_output_aliases=aliases or {},
        compiler_params=pltpu.CompilerParams(vmem_limit_bytes=limit * 2**20),
        cost_estimate=pl.CostEstimate(
            flops=flops, bytes_accessed=2**22, transcendentals=2**19
        ),
    )(*args)


def per_device(images, references, initial_contrast):
    count, width = images.shape
    refs = references.shape[0]
    devices = lax.axis_size("ref")
    f32, bf16 = jnp.float32, jnp.bfloat16
    per_image = (count // LANES, LANES)
    prior = initial_contrast.reshape(per_image)
    two = pltpu.VMEM((devices, 2 * per_image[0], LANES), f32)
    one = pltpu.VMEM((devices, *per_image), f32)
    flops = 2 * count * refs * width

    cross, kept, norms, own = call(
        first_kernel,
        (
            pltpu.VMEM((refs, count), f32),
            pltpu.VMEM((count, width), bf16),
            pltpu.VMEM((refs, LANES), f32),
            two,
        ),
        images,
        references,
        prior,
        ins=[HBM, HBM, VMEM],
        scratch=[pltpu.VMEM((refs, width), bf16), pltpu.SemaphoreType.DMA((3,))],
        limit=54,
        flops=flops,
    )
    for _ in range(ITERS - 1):
        (own,) = call(refit_kernel, (two,), exchanged(own, "ref"), cross, norms, prior, kept)
    contrast, own, fitted = call(
        total_kernel,
        (pltpu.VMEM(per_image, f32), one, pltpu.HBM(per_image, f32)),
        exchanged(own, "ref"),
        cross,
        norms,
        kept,
        specs=(VMEM, VMEM, HBM),
        scratch=[pltpu.SemaphoreType.DMA],
    )
    (img_partial,) = call(
        sum_kernel,
        (pltpu.VMEM((refs, width), bf16),),
        exchanged(own, "ref"),
        cross,
        norms,
        contrast,
        kept,
        scratch=[pltpu.VMEM((refs, count), bf16)],
        flops=flops,
    )
    share = normalize(summed_share(img_partial))
    rows = sent_to_all(share, PLANE, SPREAD).reshape(-1, width)
    first, second, last = (lax.ppermute(rows, PLANE, toward(*way)) for way in WAYS)
    norm = [pltpu.VMEM((rows.shape[0], LANES), f32)]
    log = (pltpu.VMEM(per_image, f32),)
    (before,) = call(score_kernel, log, rows, kept, contrast, scratch=norm, flops=flops // 4)
    before, begun = call(
        pair_kernel,
        (*log, pltpu.HBM((refs, width), bf16)),
        rows,
        first,
        second,
        kept,
        contrast,
        before,
        specs=(VMEM, HBM),
        scratch=[*norm, pltpu.SemaphoreType.DMA((3,))],
        flops=flops // 2,
    )
    own, new_references = call(
        last_kernel,
        (one, pltpu.HBM((refs, width), bf16)),
        last,
        kept,
        contrast,
        before,
        begun,
        ins=[VMEM] * 4 + [HBM],
        specs=(VMEM, HBM),
        scratch=[*norm, pltpu.SemaphoreType.DMA((1,))],
        aliases={4: 1},
        flops=flops // 4,
    )
    loglik = combined_log(exchanged(own, "ref")) - math.log(refs * devices)
    return (new_references, fitted.reshape(count), loglik.reshape(count))


def solution(mesh):
    placed = (P("img", None), P("ref", None), P("img"))
    return jax.shard_map(
        per_device,
        mesh=mesh,
        in_specs=placed,
        out_specs=(P("ref", None), P("img"), P("img")),
        check_vma=False,
    )
```

```python
import math

import jax
import jax.numpy as jnp
from jax import lax
from jax.experimental import pallas as pl
from jax.experimental.pallas import tpu as pltpu
from jax.sharding import PartitionSpec as P

ITERS = 3


sharpness = 2.0
prior_weight = 1.0
epsilon = 1e-06

X, Y, Z, CORES = 4, 8, 8, 2
PLANE = ("img", "ref")


def device(x, y, ref):
    return ((x % X) * Y + y % Y) * Z * CORES + ref


SIDES = [(a, b) for a in range(2) for b in range(2)]
REFS = range(Z * CORES)
BLOCKS = [
    [device(2 * i + a + ref % CORES, 2 * j + b + ref % CORES, ref) for a, b in SIDES]
    for ref in REFS
    for i in range(X // 2)
    for j in range(Y // 2)
]
ORDER = [(k % 2, (k // 2 + k % 2 * 2) % 4) for k in range(X * Y // 4)]
SPREAD = [[device(2 * i + a, 2 * j + b, ref) for i, j in ORDER] for ref in REFS for a, b in SIDES]


def exchanged(pieces, axis, groups=None):
    return lax.all_to_all(pieces, axis, 0, 0, tiled=True, axis_index_groups=groups)


def sent_to_all(value, axis, groups):
    return exchanged(jnp.broadcast_to(value[None], (len(groups[0]), *value.shape)), axis, groups)


def summed_share(partial):
    rows, width = partial.shape
    for groups in (BLOCKS, SPREAD):
        rows //= len(groups[0])
        pieces = partial.astype(jnp.bfloat16).reshape(len(groups[0]), rows, width)
        partial = jnp.sum(exchanged(pieces, PLANE, groups).astype(jnp.float32), axis=0)
    return partial


WAYS = ((0, 1), (1, 0), (1, 1))


def toward(along_x, along_y):
    pairs = []
    for ref in REFS:
        for x in range(X):
            for y in range(Y):
                a, b = (x + ref) % 2, (y + ref) % 2
                to = device(x + along_x * (1 - 2 * a), y + along_y * (1 - 2 * b), ref)
                pairs.append((device(x, y, ref), to))
    return pairs


def normalize(sums):
    meansq = jnp.mean(sums * sums, axis=1)
    return (sums * lax.rsqrt(meansq + epsilon)[:, None]).astype(jnp.bfloat16)


LANES = 128
BLOCK = 256
ROWS = BLOCK // LANES


def laid_out(value, k):
    return jnp.concatenate([value[k * ROWS + j : k * ROWS + j + 1] for j in range(ROWS)], axis=1)


def folded(parts):
    rows = [part[:, j * LANES : (j + 1) * LANES] for part in parts for j in range(ROWS)]
    return jnp.concatenate(rows, axis=0)


def block_at(k):
    return slice(k * BLOCK, (k + 1) * BLOCK)


def scored(terms, norms, contrast):
    wide = jnp.concatenate([norms[...]] * ROWS, axis=1)
    return sharpness * contrast * terms - 0.5 * sharpness * (contrast * contrast) * wide, wide


def own_refit(terms, norms, contrast, prior):
    scores, wide = scored(terms, norms, contrast)
    high = jnp.max(scores, axis=0, keepdims=True)
    e = jnp.exp(scores - high)
    total = jnp.sum(e, axis=0, keepdims=True)
    upper = jnp.sum(e * terms, axis=0, keepdims=True) + prior_weight * prior * total
    lower = jnp.sum(e * wide, axis=0, keepdims=True) + prior_weight * total
    return high + jnp.log(lower), upper / lower


def own_total(terms, norms, contrast):
    scores, _ = scored(terms, norms, contrast)
    high = jnp.max(scores, axis=0, keepdims=True)
    return high + jnp.log(jnp.sum(jnp.exp(scores - high), axis=0, keepdims=True))


def combined(received):
    logs, quotients = received[:, :8], received[:, 8:]
    share = jnp.exp(logs - jnp.max(logs, axis=0, keepdims=True))
    return jnp.sum(share * quotients, axis=0) / jnp.sum(share, axis=0)


def combined_log(logs):
    high = jnp.max(logs, axis=0)
    return high + jnp.log(jnp.sum(jnp.exp(logs - high[None]), axis=0))


def send(out, *parts):
    own = jnp.concatenate([folded(part) for part in parts], axis=0)
    out[...] = jnp.broadcast_to(own[None], out.shape)


def squares(held, norms, scale):
    rows = 64
    for i in range(held.shape[0] // rows):
        at = slice(i * rows, (i + 1) * rows)
        summed = jnp.zeros((rows, LANES), jnp.float32)
        for k in range(held.shape[1] // LANES):
            wide = held[at, k * LANES : (k + 1) * LANES].astype(jnp.float32)
            summed = summed + wide * wide
        norm = jnp.sum(summed, axis=1, keepdims=True) * scale
        norms[at, :] = jnp.broadcast_to(norm, (rows, LANES))


def product(held, images, k):
    return lax.dot_general(
        held[...], images[block_at(k), :], (((1,), (1,)), ((), ())), preferred_element_type=jnp.float32
    )


def first_kernel(images, references, prior, cross, kept, norms, out, held, semaphores):
    halves = 2
    size = images.shape[0] // halves
    copies = [pltpu.make_async_copy(references, held, semaphores.at[halves])]
    for h in range(halves):
        at = pl.ds(h * size, size)
        copies.append(pltpu.make_async_copy(images.at[at], kept.at[at], semaphores.at[h]))
    for copy in copies:
        copy.start()
    copies[0].wait()
    logs, quotients = [], []
    for h in range(halves):
        copies[h + 1].wait()
        if h == 0:
            squares(held, norms, 1.0)
        blocks = range(h * size // BLOCK, (h + 1) * size // BLOCK)
        for k in blocks:
            cross[:, block_at(k)] = product(held, kept, k)
        for k in blocks:
            start = laid_out(prior, k)
            log, quotient = own_refit(cross[:, block_at(k)], norms, start, start)
            logs.append(log)
            quotients.append(quotient)
    send(out, logs, quotients)


def refit_kernel(received, cross, norms, prior, images, out):
    contrast = combined(received[...])
    logs, quotients = [], []
    for k in range(cross.shape[1] // BLOCK):
        log, quotient = own_refit(
            cross[:, block_at(k)], norms, laid_out(contrast, k), laid_out(prior, k)
        )
        logs.append(log)
        quotients.append(quotient)
    send(out, logs, quotients)


def total_kernel(received, cross, norms, images, contrast, out, result, semaphore):
    found = combined(received[...])
    contrast[...] = found
    copy = pltpu.make_async_copy(contrast, result, semaphore)
    copy.start()
    send(
        out,
        [
            own_total(cross[:, block_at(k)], norms, laid_out(found, k))
            for k in range(cross.shape[1] // BLOCK)
        ],
    )
    copy.wait()


def sum_kernel(received, cross, norms, contrast, images, out, weights):
    log_total = combined_log(received[...])
    for k in range(cross.shape[1] // BLOCK):
        scale = laid_out(contrast, k)
        scores, _ = scored(cross[:, block_at(k)], norms, scale)
        posterior = jnp.exp(scores - laid_out(log_total, k))
        weights[:, block_at(k)] = (posterior * scale).astype(jnp.bfloat16)
    width = 512
    for k in range(images.shape[1] // width):
        at = slice(k * width, (k + 1) * width)
        out[:, at] = jnp.dot(
            weights[...], images[:, at], preferred_element_type=jnp.float32
        ).astype(jnp.bfloat16)


def scored_rows(piece, images, contrast, norms):
    width = piece.shape[1]
    squares(piece, norms, 1.0 / width)
    logs = []
    for k in range(images.shape[0] // BLOCK):
        terms = product(piece, images, k) * width**-0.5
        logs.append(own_total(terms, norms, laid_out(contrast, k)))
    return folded(logs)


def score_kernel(piece, images, contrast, out, norms):
    out[...] = scored_rows(piece, images, contrast, norms)


def writes(pieces, result, semaphores):
    image, ref = lax.axis_index("img"), lax.axis_index("ref")
    a = lax.rem(lax.div(image, Y) + ref, 2)
    b = lax.rem(lax.rem(image, Y) + ref, 2)
    copies = []
    for k, (piece, (along_x, along_y)) in enumerate(pieces):
        side = (1 - a if along_x else a) * 2 + (1 - b if along_y else b)
        rows = piece.shape[0]
        place = pl.ds(pl.multiple_of(side * rows, rows), rows)
        copies.append(pltpu.make_async_copy(piece, result.at[place], semaphores.at[k]))
    return copies


def pair_kernel(own, first, second, images, contrast, before, out, result, norms, semaphores):
    copies = writes(((own, (0, 0)), (first, WAYS[0]), (second, WAYS[1])), result, semaphores)
    for copy in copies:
        copy.start()
    logs = [before[...]]
    logs += [scored_rows(piece, images, contrast, norms) for piece in (first, second)]
    out[...] = combined_log(jnp.stack(logs))
    for copy in copies:
        copy.wait()


def last_kernel(last, images, contrast, before, begun, out, result, norms, semaphores):
    (copy,) = writes(((last, WAYS[2]),), result, semaphores)
    copy.start()
    logs = scored_rows(last, images, contrast, norms)
    out[...] = jnp.broadcast_to(combined_log(jnp.stack([before[...], logs]))[None], out.shape)
    copy.wait()


VMEM = pl.BlockSpec(memory_space=pltpu.VMEM)
HBM = pl.BlockSpec(memory_space=pltpu.HBM)


def call(kernel, outs, *args, ins=None, specs=None, scratch=(), limit=16, flops=0, aliases=None):
    return pl.pallas_call(
        kernel,
        out_shape=outs,
        in_specs=ins or [VMEM] * len(args),
        out_specs=specs or (VMEM,) * len(outs),
        scratch_shapes=scratch,
        input_output_aliases=aliases or {},
        compiler_params=pltpu.CompilerParams(vmem_limit_bytes=limit * 2**20),
        cost_estimate=pl.CostEstimate(
            flops=flops, bytes_accessed=2**22, transcendentals=2**19
        ),
    )(*args)


def per_device(images, references, initial_contrast):
    count, width = images.shape
    refs = references.shape[0]
    devices = lax.axis_size("ref")
    f32, bf16 = jnp.float32, jnp.bfloat16
    per_image = (count // LANES, LANES)
    prior = initial_contrast.reshape(per_image)
    two = pltpu.VMEM((devices, 2 * per_image[0], LANES), f32)
    one = pltpu.VMEM((devices, *per_image), f32)
    flops = 2 * count * refs * width

    cross, kept, norms, own = call(
        first_kernel,
        (
            pltpu.VMEM((refs, count), f32),
            pltpu.VMEM((count, width), bf16),
            pltpu.VMEM((refs, LANES), f32),
            two,
        ),
        images,
        references,
        prior,
        ins=[HBM, HBM, VMEM],
        scratch=[pltpu.VMEM((refs, width), bf16), pltpu.SemaphoreType.DMA((3,))],
        limit=54,
        flops=flops,
    )
    for _ in range(ITERS - 1):
        (own,) = call(refit_kernel, (two,), exchanged(own, "ref"), cross, norms, prior, kept)
    contrast, own, fitted = call(
        total_kernel,
        (pltpu.VMEM(per_image, f32), one, pltpu.HBM(per_image, f32)),
        exchanged(own, "ref"),
        cross,
        norms,
        kept,
        specs=(VMEM, VMEM, HBM),
        scratch=[pltpu.SemaphoreType.DMA],
    )
    (img_partial,) = call(
        sum_kernel,
        (pltpu.VMEM((refs, width), bf16),),
        exchanged(own, "ref"),
        cross,
        norms,
        contrast,
        kept,
        scratch=[pltpu.VMEM((refs, count), bf16)],
        flops=flops,
    )
    share = normalize(summed_share(img_partial))
    rows = sent_to_all(share, PLANE, SPREAD).reshape(-1, width)
    first, second, last = (lax.ppermute(rows, PLANE, toward(*way)) for way in WAYS)
    norm = [pltpu.VMEM((rows.shape[0], LANES), f32)]
    log = (pltpu.VMEM(per_image, f32),)
    (before,) = call(score_kernel, log, rows, kept, contrast, scratch=norm, flops=flops // 4)
    before, begun = call(
        pair_kernel,
        (*log, pltpu.HBM((refs, width), bf16)),
        rows,
        first,
        second,
        kept,
        contrast,
        before,
        specs=(VMEM, HBM),
        scratch=[*norm, pltpu.SemaphoreType.DMA((3,))],
        flops=flops // 2,
    )
    own, new_references = call(
        last_kernel,
        (one, pltpu.HBM((refs, width), bf16)),
        last,
        kept,
        contrast,
        before,
        begun,
        ins=[VMEM] * 4 + [HBM],
        specs=(VMEM, HBM),
        scratch=[*norm, pltpu.SemaphoreType.DMA((1,))],
        aliases={4: 1},
        flops=flops // 4,
    )
    loglik = combined_log(exchanged(own, "ref")) - math.log(refs * devices)
    return (new_references, fitted.reshape(count), loglik.reshape(count))


def solution(mesh):
    placed = (P("img", None), P("ref", None), P("img"))
    return jax.shard_map(
        per_device,
        mesh=mesh,
        in_specs=placed,
        out_specs=(P("ref", None), P("img"), P("img")),
        check_vma=False,
    )
```
